512 devices in a mesh: wrap: 32 (over z, y_hi), normal: 16 (over y_lo, x, core).
Axes of the slice: x: 4, y: 4 (y_hi: 2, y_lo: 2; y = y_hi * 2 + y_lo), z: 16, core: 2. Of those that a mesh axis runs over, the one named last changes fastest.
Arguments:
- adjoint_in: bfloat16 [3, 32, 1024, 2048], P(None, None, 'wrap', 'normal'), may hold values from -6 to 6
- coef: float32 [1024, 2048], P('wrap', 'normal'), may hold values from 0.08 to 0.24
- spacing: float32 [1024, 2048], P('wrap', 'normal'), may hold values from 0.5 to 288, as said below
Outputs:
- adjoint_out: bfloat16 [3, 32, 1024, 2048], P(None, None, 'wrap', 'normal')
- wall_sens: float32 [3, 32, 1024], P(None, 'normal', 'wrap')
The draws below stay inside these ranges and needn't reach their ends.
Inputs may be any that keep to these rules, and one draw needn't show every extreme that they name: `spacing`: positive arc lengths.
All inputs are finite; a program needn't handle non-finite values.
Results may differ from the reference program's by a relative error of at most 0.001.
Values sent between devices are 32-bit elements; how exact they have to be, the bound alone decides.
No kernel may reach another device: no remote copies, remote signals or barrier semaphores. Data moves between devices by JAX's collectives and lax.ppermute only.
A program may use at most 64 MiB of HBM per device.

```python
import math
import jax
import jax.numpy as jnp
from jax import lax

SWEEPS = 4
K = 32
NI = 1024
NJ = 2048


def draw_spacing(key, part):
    key = jax.random.fold_in(key, 11)
    key_base, key_rough = jax.random.split(key, 2)
    growth = 3.0
    base_top = 10.0
    rough = jnp.exp(jax.random.uniform(key_rough, (NI, NJ), jnp.float32, math.log(0.5), math.log(2.0)))
    base = jnp.exp(jax.random.uniform(key_base, (NI, 1), jnp.float32, 0.0, math.log(base_top)))
    ramp = jnp.exp(math.log(growth) * jnp.arange(NJ, dtype=jnp.float32) / (NJ - 1))
    return (base * ramp[None, :] * rough).astype(jnp.float32)


def shard_levels(own_key, dims, cuts, low, top_value):
    factor_of, own = 1.0, jax.random.fold_in(own_key, 6)
    for dim, blocks in cuts:
        steps = jnp.exp(jax.random.uniform(jax.random.fold_in(own, dim), (blocks,), jnp.float32, low / len(cuts), top_value / len(cuts)))
        factor_of = factor_of * jnp.repeat(steps, dims[dim] // blocks).reshape([-1 if axis == dim else 1 for axis in range(len(dims))])
    return factor_of


def scatter_about(stream_key, dims, width, reach, pieces=(), held_as=jnp.bfloat16):
    values = jax.random.normal(stream_key, dims, jnp.float32) * width
    if len(pieces) > 0:
        values = shard_levels(stream_key, dims, pieces, -0.22, 0.18) * values
    return jnp.clip(values, min=-reach, max=reach).astype(held_as)


def setup_inputs(seed: int = 0) -> dict:
    key_of = jax.random.split(jax.random.key(seed), 4)
    return {
        "adjoint_in": scatter_about(key_of[0], (3, K, NI, NJ), 1.0, 6.0, ((2, 32), (3, 16))),
        "coef": jnp.clip(0.08 + 0.16 * jax.random.uniform(key_of[1], (NI, NJ), jnp.float32) ** shard_levels(key_of[1], (NI, NJ), ((0, 32), (1, 16)), -0.2, 0.2), 0.08, 0.24),
        "spacing": draw_spacing(jax.random.fold_in(key_of[3], 71), 0),
    }


def smooth_slice(current, coef, interior):
    for repeat in range(SWEEPS):
        weighted = interior * coef * current
        padded = jnp.pad(weighted, ((0, 0), (1, 1)))
        current = current + jnp.roll(weighted, 1, 0) + jnp.roll(weighted, -1, 0) + padded[:, 2:] + padded[:, :-2] - 4.0 * weighted
    return current

def reference(adjoint_in, coef, spacing):
    column = jnp.arange(NJ)
    interior = ((column > 0) & (column < NJ - 1)).astype(jnp.float32)[None, :]
    line_total = lax.optimization_barrier(jnp.sum(spacing, axis=1, keepdims=True))
    before = jnp.cumsum(spacing, axis=1) - spacing
    weight = (1.0 - before / line_total) * spacing / line_total * jnp.sqrt(jnp.float32(NJ))
    flattened = adjoint_in.reshape(3 * K, NI, NJ)

    def single_slice(slice_in):
        current = smooth_slice(slice_in.astype(jnp.float32), coef, interior)
        return (current.astype(jnp.bfloat16), lax.optimization_barrier(jnp.sum(current * weight, axis=1)))
    smoothed, wall_sens = lax.map(single_slice, flattened)
    return (smoothed.reshape(3, K, NI, NJ), wall_sens.reshape(3, K, NI))
```

```python
import math

import jax
import jax.numpy as jnp
from jax import lax
from jax.experimental import pallas as pl
from jax.experimental.pallas import tpu as pltpu
from jax.sharding import PartitionSpec as P

SWEEPS = 4
HALO = 4
PLANES = 96
ROWS = 32
COLS = 128
ALL_ROWS = ROWS + 2 * HALO
ALL_COLS = COLS + 2 * HALO
MSG = HALO * PLANES + HALO * 2 * HALO + 8
F32 = jnp.float32
BF16 = jnp.bfloat16
VMEM = pl.BlockSpec(memory_space=pltpu.VMEM)


def nt(a, b):
    return lax.dot_general(a, b, (((1,), (1,)), ((), ())), preferred_element_type=F32)


def iota(shape, dim):
    return lax.broadcasted_iota(jnp.int32, shape, dim)


def call(kernel, outs, scratch, cost):
    single = not isinstance(outs, (list, tuple))
    return pl.pallas_call(
        kernel,
        out_shape=outs,
        out_specs=VMEM if single else [VMEM] * len(outs),
        scratch_shapes=scratch,
        compiler_params=pltpu.CompilerParams(vmem_limit_bytes=40 * 1024 * 1024),
        cost_estimate=pl.CostEstimate(flops=cost, bytes_accessed=2_000_000, transcendentals=0),
    )


def edge_kernel(x_ref, coef_ref, left_ref, right_ref, top_ref, bottom_ref, xf):
    xf[...] = x_ref[...].astype(F32).reshape(PLANES * ROWS, COLS)
    row, col = iota((2 * HALO, COLS), 0), iota((2 * HALO, COLS), 1)
    pick = (col == jnp.where(row < HALO, row, COLS - 2 * HALO + row)).astype(BF16)
    coef = coef_ref[...]
    coef_t = jnp.transpose(coef)
    ends = jnp.concatenate([coef_t[:HALO], coef_t[COLS - HALO :]], axis=0)
    pad = jnp.zeros((COLS - PLANES, COLS), BF16)
    lane = iota((2 * HALO, COLS), 1)
    for i in range(ROWS):
        planes = xf[pl.ds(i, PLANES, stride=ROWS), :]
        strip = nt(pick, jnp.concatenate([planes.astype(BF16), pad], axis=0))
        strip = jnp.where(lane < PLANES, strip, jnp.broadcast_to(ends[:, i : i + 1], (2 * HALO, COLS)))
        left_ref[i] = strip[:HALO]
        right_ref[i] = strip[HALO:]
        if i < HALO:
            top_ref[pl.ds(i * PLANES, PLANES), :] = planes
        if i >= ROWS - HALO:
            bottom_ref[pl.ds((i - ROWS + HALO) * PLANES, PLANES), :] = planes
    zero = jnp.zeros((HALO, COLS), F32)
    top_ref[pl.ds(MSG - 8, 8), :] = jnp.concatenate([coef[:HALO], zero], axis=0)
    bottom_ref[pl.ds(MSG - 8, 8), :] = jnp.concatenate([coef[ROWS - HALO :], zero], axis=0)
    for ref in (top_ref, bottom_ref):
        ref[pl.ds(HALO * PLANES, 8 * HALO), :] = jnp.zeros((8 * HALO, COLS), F32)


def corner_kernel(from_left, from_right, top_in, bottom_in, top_ref, bottom_ref):
    top_ref[...] = top_in[...]
    bottom_ref[...] = bottom_in[...]
    for r in range(HALO):
        at = HALO * PLANES + 8 * r
        for ref, i in ((top_ref, r), (bottom_ref, ROWS - HALO + r)):
            ref[pl.ds(at, 8), :] = jnp.concatenate([from_right[i], from_left[i]], axis=0)


def split(value):
    high = value.astype(BF16).astype(F32)
    return high, value - high


def main_kernel(x_ref, coef_ref, spacing_ref, from_left, from_right, above, below, out_ref, sums_ref, xf, v, f, sums):
    place = lax.axis_index("normal")
    last = lax.axis_size("normal") - 1
    xf[...] = x_ref[...].astype(F32).reshape(PLANES * ROWS, COLS)
    eye = (iota((COLS, COLS), 0) == iota((COLS, COLS), 1)).astype(BF16)
    pad = jnp.zeros((COLS - PLANES, COLS), BF16)
    at = HALO * PLANES + 8 * HALO
    coef_all = jnp.concatenate(
        [above[pl.ds(at, HALO), :], coef_ref[...], below[pl.ds(at, HALO), :], jnp.zeros((COLS - ALL_ROWS, COLS), F32)],
        axis=0,
    )
    coef_t = jnp.transpose(coef_all)
    own_col = iota((COLS, COLS), 0)
    inside = jnp.logical_not(((own_col == 0) & (place == 0)) | ((own_col == COLS - 1) & (place == last)))
    coef_t = jnp.where(inside, coef_t, 0.0)
    for r in range(ALL_ROWS):
        if r < HALO:
            planes = above[pl.ds(r * PLANES, PLANES), :]
            strip = above[pl.ds(HALO * PLANES + 8 * r, 8), :]
        elif r < HALO + ROWS:
            planes = xf[pl.ds(r - HALO, PLANES, stride=ROWS), :]
            strip = jnp.concatenate([from_right[r - HALO], from_left[r - HALO]], axis=0)
        else:
            k = r - HALO - ROWS
            planes = below[pl.ds(k * PLANES, PLANES), :]
            strip = below[pl.ds(HALO * PLANES + 8 * k, 8), :]
        v[r, pl.ds(0, COLS), :] = nt(eye, jnp.concatenate([planes.astype(BF16), pad], axis=0))
        v[r, pl.ds(COLS, 8), :] = strip
        f[r, pl.ds(0, COLS), :] = jnp.broadcast_to(coef_t[:, r : r + 1], (COLS, COLS))
        f[r, pl.ds(COLS, 8), :] = jnp.broadcast_to(strip[:, PLANES : PLANES + 1], (8, COLS))

    for sweep in range(SWEEPS):

        def update(r, held):
            before, here = held
            after = f[r + 1] * v[r + 1]
            beside = pltpu.roll(here, 1, 0) + pltpu.roll(here, ALL_COLS - 1, 0)
            v[r] = (v[r] - 4.0 * here) + ((before + after) + beside)
            return here, after

        lax.fori_loop(sweep + 1, ALL_ROWS - 1 - sweep, update, (f[sweep] * v[sweep], f[sweep + 1] * v[sweep + 1]))

    spacing = spacing_ref[...]
    earlier = (iota((COLS, COLS), 0) < iota((COLS, COLS), 1)).astype(F32)
    before = lax.dot_general(
        spacing, earlier, (((1,), (0,)), ((), ())), preferred_element_type=F32, precision=lax.Precision.HIGHEST
    )
    s_high, s_low = split(spacing)
    q_high, q_low = split(before * spacing)
    sums[pl.ds(2 * ROWS, ROWS), :] = jnp.broadcast_to(jnp.sum(spacing, axis=1, keepdims=True), (ROWS, COLS))
    sums[pl.ds(3 * ROWS, ROWS), :] = jnp.zeros((ROWS, COLS), F32)
    place16 = iota((16, COLS), 0)
    for i in range(ROWS):
        value = v[HALO + i, pl.ds(0, COLS), :]
        high = value.astype(BF16)
        low = (value - high.astype(F32)).astype(BF16)
        rows = [jnp.broadcast_to(a[i : i + 1], (16, COLS)) for a in (s_high, q_high, s_low, q_low)]
        weight = jnp.where(
            place16 == 0,
            rows[0],
            jnp.where(place16 == 1, rows[1], jnp.where(place16 == 2, rows[2], jnp.where(place16 == 3, rows[3], 0.0))),
        ).astype(BF16)
        both = lax.dot_general(weight, high, (((1,), (0,)), ((), ())), preferred_element_type=F32) + lax.dot_general(
            weight, low, (((1,), (0,)), ((), ())), preferred_element_type=F32
        )
        sums[pl.ds(i, 1), :] = both[0:1] + both[2:3]
        sums[pl.ds(ROWS + i, 1), :] = both[1:2] + both[3:4]
        xf[pl.ds(i, PLANES, stride=ROWS), :] = nt(eye[:PLANES], high)
    out_ref[...] = xf[...].astype(BF16).reshape(PLANES, ROWS, COLS)
    sums[...] = jnp.transpose(sums[...])
    owners = sums_ref.shape[0]
    each = ROWS // owners
    for c in range(3):
        for e in range(each):
            sums_ref[:, c * each + e, :] = sums[pl.ds(c * ROWS + e, owners, stride=each), :]
    sums_ref[:, 3 * each :, :] = jnp.zeros((owners, 8 - 3 * each, COLS), F32)


def owner_kernel(got_ref, out_ref):
    owners = got_ref.shape[0]
    each = ROWS // owners
    own = [pltpu.roll(got_ref[d], COLS - 2 * ROWS, 1) for d in range(owners)]
    total = own[0]
    for d in range(1, owners):
        total = total + own[d]
    rest = total
    acc = jnp.zeros_like(total)
    moment = jnp.zeros_like(total)
    for d in range(owners):
        acc = acc + got_ref[d] * rest
        moment = moment + got_ref[d]
        rest = rest - own[d]
    acc = acc - pltpu.roll(moment, COLS - ROWS, 1)
    value = (acc / total) / total * math.sqrt(COLS * owners)
    for c in range(3):
        out_ref[c] = value[c * each : (c + 1) * each, :ROWS]


def body(adjoint_in, coef, spacing):
    wraps, owners = lax.axis_size("wrap"), lax.axis_size("normal")
    x = adjoint_in.reshape(PLANES, ROWS, COLS)
    strip = jax.ShapeDtypeStruct((ROWS, HALO, COLS), F32)
    message = jax.ShapeDtypeStruct((MSG, COLS), F32)
    left, right, top, bottom = call(
        edge_kernel, [strip, strip, message, message], [pltpu.VMEM((PLANES * ROWS, COLS), F32)], 10_000_000
    )(x, coef)
    from_left = lax.ppermute(right, "normal", [(k, k + 1) for k in range(owners - 1)])
    from_right = lax.ppermute(left, "normal", [(k + 1, k) for k in range(owners - 1)])
    top, bottom = call(corner_kernel, [message, message], [], 1_000_000)(from_left, from_right, top, bottom)
    above = lax.ppermute(bottom, "wrap", [(k, (k + 1) % wraps) for k in range(wraps)])
    below = lax.ppermute(top, "wrap", [((k + 1) % wraps, k) for k in range(wraps)])
    adjoint_out, sums = call(
        main_kernel,
        [jax.ShapeDtypeStruct((PLANES, ROWS, COLS), BF16), jax.ShapeDtypeStruct((owners, 8, COLS), F32)],
        [
            pltpu.VMEM((PLANES * ROWS, COLS), F32),
            pltpu.VMEM((ALL_ROWS, ALL_COLS, COLS), F32),
            pltpu.VMEM((ALL_ROWS, ALL_COLS, COLS), F32),
            pltpu.VMEM((COLS, COLS), F32),
        ],
        50_000_000,
    )(x, coef, spacing, from_left, from_right, above, below)
    got = lax.all_to_all(sums, "normal", 0, 0, tiled=True)
    wall_sens = call(owner_kernel, jax.ShapeDtypeStruct((3, ROWS // owners, ROWS), F32), [], 100_000)(got)
    return adjoint_out.reshape(3, PLANES // 3, ROWS, COLS), wall_sens


def solution(mesh):
    placed = (P(None, None, "wrap", "normal"), P("wrap", "normal"), P("wrap", "normal"))
    return jax.shard_map(
        body,
        mesh=mesh,
        in_specs=placed,
        out_specs=(P(None, None, "wrap", "normal"), P(None, "normal", "wrap")),
        check_vma=False,
    )
```

```python
import math

import jax
import jax.numpy as jnp
from jax import lax
from jax.experimental import pallas as pl
from jax.experimental.pallas import tpu as pltpu
from jax.sharding import PartitionSpec as P

SWEEPS = 4
HALO = 4
PLANES = 96
LAYER = 32
ROWS = 32
COLS = 128
WIDE = COLS + 2 * HALO
STEPS = WIDE // 8
STRIP_AT = WIDE - 7 * 8 - 1
STRIPS = HALO * PLANES
COEFS = STRIPS + 8 * HALO
MSG = COEFS + 8
F32 = jnp.float32
BF16 = jnp.bfloat16
COEF_AT = PLANES * ROWS
SPACING_AT = COEF_AT + ROWS
ALL = SPACING_AT + ROWS
VMEM = pl.BlockSpec(memory_space=pltpu.VMEM)


def nt(a, b):
    return lax.dot_general(a, b, (((1,), (1,)), ((), ())), preferred_element_type=F32)


def iota(shape, dim):
    return lax.broadcasted_iota(jnp.int32, shape, dim)


def call(kernel, ins, outs, scratch, cost, aliases=None):
    single = not isinstance(outs, (list, tuple))
    return pl.pallas_call(
        kernel,
        in_specs=[VMEM] * ins,
        out_shape=outs,
        out_specs=VMEM if single else [VMEM] * len(outs),
        scratch_shapes=scratch,
        input_output_aliases=aliases or {},
        compiler_params=pltpu.CompilerParams(vmem_limit_bytes=24 * 1024 * 1024),
        cost_estimate=pl.CostEstimate(flops=cost, bytes_accessed=2_000_000, transcendentals=0),
    )


def ring(line):
    return 17 * (line & 7) + (line >> 3)


def line_of(ref, r):
    return ref[pl.ds(pl.multiple_of(r * WIDE, 8), WIDE), :].reshape(STEPS, 8, COLS)


def put_line(ref, r, value):
    ref[pl.ds(pl.multiple_of(r * WIDE, 8), WIDE), :] = value.reshape(WIDE, COLS)


def put_plain(ref, r, value):
    for q in range(STEPS):
        ref[pl.ds(r * WIDE + q, 8, stride=STEPS), :] = value[q]


def put_strip(ref, r, strip):
    ref[pl.ds(r * WIDE + STRIP_AT, 8, stride=8), :] = strip


def opened(value, here, before):
    first = pltpu.roll(here[STEPS - 1], 1, 0)[None]
    last = pltpu.roll(here[0], 7, 0)[None]
    beside = jnp.concatenate([first, here[:-1]], axis=0) + jnp.concatenate([here[1:], last], axis=0)
    return (value - 4.0 * here) + (beside + before)


def selector():
    shape = (WIDE, COLS)
    return (ring(iota(shape, 0)) == iota(shape, 1)).astype(BF16)


def to_lanes(select, planes):
    pad = jnp.zeros((COLS - PLANES, COLS), BF16)
    return nt(select, jnp.concatenate([planes.astype(BF16), pad], axis=0))


def coef_strip(strip):
    return jnp.broadcast_to(strip[:, PLANES : PLANES + 1], (8, COLS))


def masked_ring(coef, scratch):
    rows = coef.shape[0]
    coef_t = jnp.transpose(jnp.concatenate([coef, jnp.zeros((COLS - rows, COLS), F32)], axis=0))
    place, last = lax.axis_index("normal"), lax.axis_size("normal") - 1
    col = iota((COLS, COLS), 0)
    outer = ((col == 0) & (place == 0)) | ((col == COLS - 1) & (place == last))
    scratch[pl.ds(0, COLS), :] = jnp.where(outer, 0.0, coef_t)
    scratch[pl.ds(COLS, 8), :] = jnp.zeros((8, COLS), F32)
    return jnp.concatenate([scratch[pl.ds(q, 8, stride=STEPS), :] for q in range(STEPS)], axis=0)


def line_sums(value, weight):
    high = value.astype(BF16)
    low = (value - high.astype(F32)).astype(BF16)
    both = lax.dot_general(
        jnp.concatenate([weight, weight], axis=1),
        jnp.concatenate([high, low], axis=0),
        (((1,), (0,)), ((), ())),
        preferred_element_type=F32,
    )
    return high, both[0:1] + both[2:3], both[1:2] + both[3:4]


def weight_of(weights, i):
    place = iota((16, COLS), 0)
    rows = [jnp.broadcast_to(weights[k * ROWS + i : k * ROWS + i + 1], (16, COLS)) for k in range(4)]
    rest = jnp.where(place == 2, rows[2], jnp.where(place == 3, rows[3], 0.0))
    return jnp.where(place == 0, rows[0], jnp.where(place == 1, rows[1], rest)).astype(BF16)


def split(value):
    high = value.astype(BF16).astype(F32)
    return high, value - high


def strip_kernel(all_ref, twin_ref, cross_ref, top_ref, bottom_ref):
    row, col = iota((2 * HALO, COLS), 0), iota((2 * HALO, COLS), 1)
    pick = (col == jnp.where(row < HALO, row, COLS - 2 * HALO + row)).astype(BF16)
    even = lax.axis_index("normal") % 2 == 0
    coef = all_ref[pl.ds(COEF_AT, ROWS), :]
    coef_t = jnp.transpose(jnp.concatenate([coef, jnp.zeros((COLS - ROWS, COLS), F32)], axis=0))
    ends = jnp.concatenate([coef_t[:HALO], coef_t[COLS - HALO :]], axis=0)
    pad = jnp.zeros((COLS - PLANES, COLS), BF16)
    for i in range(ROWS):
        planes = all_ref[pl.ds(i, PLANES, stride=ROWS), :]
        strip = nt(pick, jnp.concatenate([planes.astype(BF16), pad], axis=0))
        strip = jnp.where(col < PLANES, strip, jnp.broadcast_to(ends[:, i : i + 1], (2 * HALO, COLS)))
        twin_ref[i] = jnp.where(even, strip[HALO:], strip[:HALO])
        cross_ref[i] = jnp.where(even, strip[:HALO], strip[HALO:])
        if i < HALO:
            top_ref[pl.ds(i * PLANES, PLANES), :] = planes
        if i >= ROWS - HALO:
            bottom_ref[pl.ds((i - ROWS + HALO) * PLANES, PLANES), :] = planes
    zero = jnp.zeros((HALO, COLS), F32)
    top_ref[pl.ds(COEFS, 8), :] = jnp.concatenate([coef[:HALO], zero], axis=0)
    bottom_ref[pl.ds(COEFS, 8), :] = jnp.concatenate([coef[ROWS - HALO :], zero], axis=0)
    for ref in (top_ref, bottom_ref):
        ref[pl.ds(STRIPS, 8 * HALO), :] = jnp.zeros((8 * HALO, COLS), F32)


def corner_kernel(twin, cross, top_in, bottom_in, after_setup, top_ref, bottom_ref, strips_ref):
    even = lax.axis_index("normal") % 2 == 0
    right = jnp.where(even, twin[...], cross[...])
    left = jnp.where(even, cross[...], twin[...])
    strips = jnp.concatenate([right, left], axis=1)
    strips_ref[...] = strips
    top_ref[...] = top_in[...]
    bottom_ref[...] = bottom_in[...]
    for r in range(HALO):
        top_ref[pl.ds(STRIPS + 8 * r, 8), :] = strips[r]
        bottom_ref[pl.ds(STRIPS + 8 * r, 8), :] = strips[ROWS - HALO + r]


def setup_kernel(all_ref, v, f, weights, sums, ct):
    select = selector()
    ring_coef = masked_ring(all_ref[pl.ds(COEF_AT, ROWS), :], ct)
    for r in range(ROWS):
        v[pl.ds(r * WIDE, WIDE), :] = to_lanes(select, all_ref[pl.ds(r, PLANES, stride=ROWS), :])
        f[pl.ds(r * WIDE, WIDE), :] = jnp.broadcast_to(ring_coef[:, r : r + 1], (WIDE, COLS))
    spacing = all_ref[pl.ds(SPACING_AT, ROWS), :]
    earlier = (iota((COLS, COLS), 0) < iota((COLS, COLS), 1)).astype(F32)
    before = lax.dot_general(
        spacing, earlier, (((1,), (0,)), ((), ())), preferred_element_type=F32, precision=lax.Precision.HIGHEST
    )
    s_high, s_low = split(spacing)
    q_high, q_low = split(before * spacing)
    weights[...] = jnp.concatenate([s_high, q_high, s_low, q_low], axis=0)
    total = jnp.broadcast_to(jnp.sum(spacing, axis=1, keepdims=True), (ROWS, COLS))
    empty = jnp.zeros((ROWS, COLS), F32)
    sums[...] = jnp.concatenate([empty, empty, total, empty], axis=0)


def inner_kernel(v_in, f_in, strips, weights, sums_in, v, f, kept, part, sums):
    for r in range(ROWS):
        put_strip(v, r, strips[r])
        put_strip(f, r, coef_strip(strips[r]))

    for sweep in range(SWEEPS):
        put = put_line if sweep < SWEEPS - 1 else put_plain
        low, high = sweep + 1, ROWS - 2 - sweep

        def step(r, held):
            sofar, here = held
            value = line_of(v, r + 1)
            after = line_of(f, r + 1) * value
            put(v, r, sofar + after)
            return opened(value, after, here), after

        value = line_of(v, low)
        here = line_of(f, low) * value
        put_line(kept, sweep, here)
        held = (opened(value, here, line_of(f, low - 1) * line_of(v, low - 1)), here)
        held = lax.fori_loop(low, high, step, held, unroll=4)
        put_line(kept, HALO + sweep, held[1])
        put(v, high, held[0] + line_of(f, high + 1) * line_of(v, high + 1))

    sums[...] = sums_in[...]
    eye = (iota((PLANES, COLS), 0) == iota((PLANES, COLS), 1)).astype(BF16)
    for i in range(HALO, ROWS - HALO):
        high, p, q = line_sums(v[pl.ds(i * WIDE, COLS), :], weight_of(weights[...], i))
        sums[pl.ds(i, 1), :] = p
        sums[pl.ds(ROWS + i, 1), :] = q
        part[pl.ds(i, PLANES, stride=ROWS), :] = nt(eye, high)


def outer_kernel(above, below, v, f, kept, part, sums_in, weights, out_ref, send_ref, hv, hf, hw, ct, xe, plain, sums):
    select = selector()
    ring_coef = masked_ring(jnp.concatenate([above[pl.ds(COEFS, HALO), :], below[pl.ds(COEFS, HALO), :]], axis=0), ct)
    for k in range(HALO):
        for message, at, c in ((above, k, k), (below, 3 * HALO + k, HALO + k)):
            hv[pl.ds(at * WIDE, WIDE), :] = to_lanes(select, message[pl.ds(k * PLANES, PLANES), :])
            hf[pl.ds(at * WIDE, WIDE), :] = jnp.broadcast_to(ring_coef[:, c : c + 1], (WIDE, COLS))
            strip = message[pl.ds(STRIPS + 8 * k, 8), :]
            put_strip(hv, at, strip)
            put_strip(hf, at, coef_strip(strip))
    own = {HALO + k: k for k in range(HALO)} | {2 * HALO + k: ROWS - HALO + k for k in range(HALO)}
    moved = set()

    def value_of(e):
        return line_of(v, own[e]) if e in own and e not in moved else line_of(hv, e)

    def coef_of(e):
        return line_of(f, own[e]) if e in own else line_of(hf, e)

    def chain(first, before, last_after):
        value = value_of(first)
        here = coef_of(first) * value
        sofar = opened(value, here, before)
        for e in range(first, first + HALO):
            if e == first + HALO - 1 and last_after is not None:
                put_line(hv, e, sofar + last_after)
            else:
                value = value_of(e + 1)
                after = coef_of(e + 1) * value
                put_line(hv, e, sofar + after)
                if e < first + HALO - 1:
                    sofar = opened(value, after, here)
                here = after
            moved.add(e)

    for sweep in range(SWEEPS):
        chain(sweep + 1, coef_of(sweep) * value_of(sweep), line_of(kept, sweep))
        chain(3 * HALO - 1 - sweep, line_of(kept, HALO + sweep), None)
    sums[...] = sums_in[...]
    eye = (iota((PLANES, COLS), 0) == iota((PLANES, COLS), 1)).astype(BF16)
    for k in range(2 * HALO):
        i = k if k < HALO else ROWS - 2 * HALO + k
        put_plain(plain, k, line_of(hv, HALO + k))
        high, p, q = line_sums(plain[pl.ds(k * WIDE, COLS), :], weight_of(weights[...], i))
        sums[pl.ds(i, 1), :] = p
        sums[pl.ds(ROWS + i, 1), :] = q
        xe[pl.ds(k, PLANES, stride=2 * HALO), :] = nt(eye, high)
    tiles = part[...].reshape(PLANES, ROWS // 8, 8, COLS)
    ends = xe[...].reshape(PLANES, 8, COLS)
    near = iota((PLANES, 8, COLS), 1) < HALO
    head = jnp.where(near, ends, tiles[:, 0])
    tail = jnp.where(near, tiles[:, 3], ends)
    out_ref[...] = jnp.concatenate([head, tiles[:, 1], tiles[:, 2], tail], axis=1).astype(BF16)
    sums[...] = jnp.transpose(sums[...])
    owners = send_ref.shape[0]
    each = LAYER // owners
    for c in range(3):
        for e in range(each):
            send_ref[:, c * each + e, :] = sums[pl.ds(c * LAYER + e, owners, stride=each), :]
    send_ref[:, 3 * each :, :] = jnp.zeros((owners, 8 - 3 * each, COLS), F32)


def owner_kernel(got_ref, out_ref):
    owners = got_ref.shape[0]
    each = LAYER // owners
    own = [pltpu.roll(got_ref[d], COLS - 2 * ROWS, 1) for d in range(owners)]
    total = own[0]
    for d in range(1, owners):
        total = total + own[d]
    rest = total
    acc = jnp.zeros_like(total)
    moment = jnp.zeros_like(total)
    for d in range(owners):
        acc = acc + got_ref[d] * rest
        moment = moment + got_ref[d]
        rest = rest - own[d]
    acc = acc - pltpu.roll(moment, COLS - ROWS, 1)
    value = (acc / total) / total * math.sqrt(COLS * owners)
    for c in range(3):
        out_ref[c] = value[c * each : (c + 1) * each, :ROWS]


def shaped(*shape):
    return jax.ShapeDtypeStruct(shape, F32)


def lines(count):
    return pltpu.VMEM((count * WIDE, COLS), F32)


def body(adjoint_in, coef, spacing):
    wraps, owners = lax.axis_size("wrap"), lax.axis_size("normal")
    everything = jnp.concatenate([adjoint_in.reshape(PLANES * ROWS, COLS).astype(F32), coef, spacing], axis=0)
    strip, message, square = shaped(ROWS, HALO, COLS), shaped(MSG, COLS), shaped(COLS, COLS)
    own_rows = shaped(ROWS * WIDE, COLS)
    twin, cross, top, bottom = call(strip_kernel, 1, [strip, strip, message, message], [], 10_000_000)(everything)
    cross = lax.ppermute(cross, "normal", [(k, k + 1 if k % 2 else k - 1) for k in range(1, owners - 1)])
    twin = lax.ppermute(twin, "normal", [(k, k ^ 1) for k in range(owners)])
    v, f, weights, sums = call(
        setup_kernel, 1, [own_rows, own_rows, square, square], [pltpu.VMEM((WIDE, COLS), F32)], 20_000_000
    )(everything)
    top, bottom, strips = call(corner_kernel, 5, [message, message, shaped(ROWS, 8, COLS)], [], 1_000_000)(
        twin, cross, top, bottom, sums
    )
    above = lax.ppermute(bottom, "wrap", [(k, (k + 1) % wraps) for k in range(wraps)])
    below = lax.ppermute(top, "wrap", [((k + 1) % wraps, k) for k in range(wraps)])
    v, f, kept, part, sums = call(
        inner_kernel,
        5,
        [own_rows, own_rows, shaped(2 * HALO * WIDE, COLS), shaped(PLANES * ROWS, COLS), square],
        [],
        50_000_000,
        {0: 0, 1: 1},
    )(v, f, strips, weights, sums)
    adjoint_out, sums = call(
        outer_kernel,
        8,
        [jax.ShapeDtypeStruct((PLANES, ROWS, COLS), BF16), shaped(owners, 8, COLS)],
        [
            lines(4 * HALO),
            lines(4 * HALO),
            lines(1),
            pltpu.VMEM((WIDE, COLS), F32),
            pltpu.VMEM((PLANES * 2 * HALO, COLS), F32),
            lines(2 * HALO),
            pltpu.VMEM((COLS, COLS), F32),
        ],
        10_000_000,
    )(above, below, v, f, kept, part, sums, weights)
    got = lax.all_to_all(sums, "normal", 0, 0, tiled=True)
    wall_sens = call(owner_kernel, 1, shaped(3, LAYER // owners, ROWS), [], 100_000)(got)
    return adjoint_out.reshape(3, LAYER, ROWS, COLS), wall_sens


def solution(mesh):
    placed = (P(None, None, "wrap", "normal"), P("wrap", "normal"), P("wrap", "normal"))
    return jax.shard_map(
        body,
        mesh=mesh,
        in_specs=placed,
        out_specs=(P(None, None, "wrap", "normal"), P(None, "normal", "wrap")),
        check_vma=False,
    )
```

```python
import math

import jax
import jax.numpy as jnp
from jax import lax
from jax.experimental import pallas as pl
from jax.experimental.pallas import tpu as pltpu
from jax.sharding import PartitionSpec as P

SWEEPS = 4
HALO = 4
PLANES = 96
LAYER = 32
ROWS = 32
COLS = 128
WIDE = COLS + 2 * HALO
STEPS = WIDE // 8
STRIP_AT = WIDE - 7 * 8 - 1
COEFS = HALO * PLANES
MAIN = COEFS + 8
MSG = MAIN + 8 * HALO
F32 = jnp.float32
BF16 = jnp.bfloat16
COEF_AT = PLANES * ROWS
SPACING_AT = COEF_AT + ROWS
ALL = SPACING_AT + ROWS
VMEM = pl.BlockSpec(memory_space=pltpu.VMEM)


def nt(a, b):
    return lax.dot_general(a, b, (((1,), (1,)), ((), ())), preferred_element_type=F32)


def iota(shape, dim):
    return lax.broadcasted_iota(jnp.int32, shape, dim)


def call(kernel, ins, outs, scratch, cost, aliases=None):
    single = not isinstance(outs, (list, tuple))
    return pl.pallas_call(
        kernel,
        in_specs=[VMEM] * ins,
        out_shape=outs,
        out_specs=VMEM if single else [VMEM] * len(outs),
        scratch_shapes=scratch,
        input_output_aliases=aliases or {},
        compiler_params=pltpu.CompilerParams(vmem_limit_bytes=24 * 1024 * 1024),
        cost_estimate=pl.CostEstimate(flops=cost, bytes_accessed=1_000, transcendentals=0),
    )


def ring(line):
    return 17 * (line & 7) + (line >> 3)


def line_of(ref, r):
    return ref[pl.ds(pl.multiple_of(r * WIDE, 8), WIDE), :].reshape(STEPS, 8, COLS)


def put_line(ref, r, value):
    ref[pl.ds(pl.multiple_of(r * WIDE, 8), WIDE), :] = value.reshape(WIDE, COLS)


def put_plain(ref, r, value):
    for q in range(STEPS):
        ref[pl.ds(r * WIDE + q, 8, stride=STEPS), :] = value[q]


def put_strip(ref, r, strip):
    ref[pl.ds(r * WIDE + STRIP_AT, 8, stride=8), :] = strip


def opened(value, here, before):
    first = pltpu.roll(here[STEPS - 1], 1, 0)[None]
    last = pltpu.roll(here[0], 7, 0)[None]
    beside = jnp.concatenate([first, here[:-1]], axis=0) + jnp.concatenate([here[1:], last], axis=0)
    return (value - 4.0 * here) + (beside + before)


def selector():
    shape = (WIDE, COLS)
    return (ring(iota(shape, 0)) == iota(shape, 1)).astype(BF16)


def to_lanes(select, planes):
    pad = jnp.zeros((COLS - PLANES, COLS), BF16)
    return nt(select, jnp.concatenate([planes.astype(BF16), pad], axis=0))


def coef_strip(strip):
    return jnp.broadcast_to(strip[:, PLANES : PLANES + 1], (8, COLS))


def masked_ring(coef, scratch):
    rows = coef.shape[0]
    coef_t = jnp.transpose(jnp.concatenate([coef, jnp.zeros((COLS - rows, COLS), F32)], axis=0))
    place, last = lax.axis_index("normal"), lax.axis_size("normal") - 1
    col = iota((COLS, COLS), 0)
    outer = ((col == 0) & (place == 0)) | ((col == COLS - 1) & (place == last))
    scratch[pl.ds(0, COLS), :] = jnp.where(outer, 0.0, coef_t)
    scratch[pl.ds(COLS, 8), :] = jnp.zeros((8, COLS), F32)
    return jnp.concatenate([scratch[pl.ds(q, 8, stride=STEPS), :] for q in range(STEPS)], axis=0)


def line_sums(value, weight):
    high = value.astype(BF16)
    low = (value - high.astype(F32)).astype(BF16)
    both = lax.dot_general(
        jnp.concatenate([weight, weight], axis=1),
        jnp.concatenate([high, low], axis=0),
        (((1,), (0,)), ((), ())),
        preferred_element_type=F32,
    )
    return high, both[0:1] + both[2:3], both[1:2] + both[3:4]


def weight_of(weights, i):
    place = iota((16, COLS), 0)
    rows = [jnp.broadcast_to(weights[k * ROWS + i : k * ROWS + i + 1], (16, COLS)) for k in range(4)]
    rest = jnp.where(place == 2, rows[2], jnp.where(place == 3, rows[3], 0.0))
    return jnp.where(place == 0, rows[0], jnp.where(place == 1, rows[1], rest)).astype(BF16)


def split(value):
    high = value.astype(BF16).astype(F32)
    return high, value - high


def rows_kernel(all_ref, after_setup, top_ref, bottom_ref):
    zero = jnp.zeros((HALO, COLS), F32)
    for ref, at in ((top_ref, 0), (bottom_ref, ROWS - HALO)):
        for k in range(HALO):
            ref[pl.ds(k * PLANES, PLANES), :] = all_ref[pl.ds(at + k, PLANES, stride=ROWS), :]
        ref[pl.ds(COEFS, 8), :] = jnp.concatenate([all_ref[pl.ds(COEF_AT + at, HALO), :], zero], axis=0)


def strip_kernel(all_ref, cross_ref, twin_ref):
    row, col = iota((2 * HALO, COLS), 0), iota((2 * HALO, COLS), 1)
    pick = (col == jnp.where(row < HALO, row, COLS - 2 * HALO + row)).astype(BF16)
    even = lax.axis_index("normal") % 2 == 0
    coef = all_ref[pl.ds(COEF_AT, ROWS), :]
    coef_t = jnp.transpose(jnp.concatenate([coef, jnp.zeros((COLS - ROWS, COLS), F32)], axis=0))
    ends = jnp.concatenate([coef_t[:HALO], coef_t[COLS - HALO :]], axis=0)
    pad = jnp.zeros((COLS - PLANES, COLS), BF16)
    for i in range(ROWS):
        planes = all_ref[pl.ds(i, PLANES, stride=ROWS), :]
        strip = nt(pick, jnp.concatenate([planes.astype(BF16), pad], axis=0))
        strip = jnp.where(col < PLANES, strip, jnp.broadcast_to(ends[:, i : i + 1], (2 * HALO, COLS)))
        cross_ref[i] = jnp.where(even, strip[:HALO], strip[HALO:])
        twin_ref[i] = jnp.where(even, strip[HALO:], strip[:HALO])


def pass_kernel(ref, out_ref):
    out_ref[...] = ref[...]


def corner_kernel(cross, twin, top, bottom, strips_ref, top_ref, bottom_ref):
    even = lax.axis_index("normal") % 2 == 0
    right = jnp.where(even, twin[...], cross[...])
    left = jnp.where(even, cross[...], twin[...])
    strips = jnp.concatenate([right, left], axis=1)
    strips_ref[...] = strips
    top_ref[pl.ds(0, MAIN), :] = top[...]
    bottom_ref[pl.ds(0, MAIN), :] = bottom[...]
    for r in range(HALO):
        top_ref[pl.ds(MAIN + 8 * r, 8), :] = strips[r]
        bottom_ref[pl.ds(MAIN + 8 * r, 8), :] = strips[ROWS - HALO + r]


def setup_kernel(all_ref, after_strip, v, f, weights, sums, ct):
    select = selector()
    ring_coef = masked_ring(all_ref[pl.ds(COEF_AT, ROWS), :], ct)
    for r in range(ROWS):
        v[pl.ds(r * WIDE, WIDE), :] = to_lanes(select, all_ref[pl.ds(r, PLANES, stride=ROWS), :])
        f[pl.ds(r * WIDE, WIDE), :] = jnp.broadcast_to(ring_coef[:, r : r + 1], (WIDE, COLS))
    spacing = all_ref[pl.ds(SPACING_AT, ROWS), :]
    earlier = (iota((COLS, COLS), 0) < iota((COLS, COLS), 1)).astype(F32)
    before = lax.dot_general(
        spacing, earlier, (((1,), (0,)), ((), ())), preferred_element_type=F32, precision=lax.Precision.HIGHEST
    )
    s_high, s_low = split(spacing)
    q_high, q_low = split(before * spacing)
    weights[...] = jnp.concatenate([s_high, q_high, s_low, q_low], axis=0)
    total = jnp.broadcast_to(jnp.sum(spacing, axis=1, keepdims=True), (ROWS, COLS))
    empty = jnp.zeros((ROWS, COLS), F32)
    sums[...] = jnp.concatenate([empty, empty, total, empty], axis=0)


def inner_kernel(v_in, f_in, strips, weights, sums_in, v, f, kept, part, sums):
    for r in range(ROWS):
        put_strip(v, r, strips[r])
        put_strip(f, r, coef_strip(strips[r]))

    for sweep in range(SWEEPS):
        put = put_line if sweep < SWEEPS - 1 else put_plain
        low, high = sweep + 1, ROWS - 2 - sweep

        def step(r, held):
            sofar, here = held
            value = line_of(v, r + 1)
            after = line_of(f, r + 1) * value
            put(v, r, sofar + after)
            return opened(value, after, here), after

        value = line_of(v, low)
        here = line_of(f, low) * value
        put_line(kept, sweep, here)
        held = (opened(value, here, line_of(f, low - 1) * line_of(v, low - 1)), here)
        held = lax.fori_loop(low, high, step, held, unroll=4)
        put_line(kept, HALO + sweep, held[1])
        put(v, high, held[0] + line_of(f, high + 1) * line_of(v, high + 1))

    sums[...] = sums_in[...]
    eye = (iota((PLANES, COLS), 0) == iota((PLANES, COLS), 1)).astype(BF16)
    for i in range(HALO, ROWS - HALO):
        high, p, q = line_sums(v[pl.ds(i * WIDE, COLS), :], weight_of(weights[...], i))
        sums[pl.ds(i, 1), :] = p
        sums[pl.ds(ROWS + i, 1), :] = q
        part[pl.ds(i, PLANES, stride=ROWS), :] = nt(eye, high)


def outer_kernel(above, below, v, f, kept, sums_in, weights, xe, send_ref, hv, hf, ct, plain, sums):
    select = selector()
    ring_coef = masked_ring(jnp.concatenate([above[pl.ds(COEFS, HALO), :], below[pl.ds(COEFS, HALO), :]], axis=0), ct)
    for k in range(HALO):
        for message, at, c in ((above, k, k), (below, 3 * HALO + k, HALO + k)):
            hv[pl.ds(at * WIDE, WIDE), :] = to_lanes(select, message[pl.ds(k * PLANES, PLANES), :])
            hf[pl.ds(at * WIDE, WIDE), :] = jnp.broadcast_to(ring_coef[:, c : c + 1], (WIDE, COLS))
            strip = message[pl.ds(MAIN + 8 * k, 8), :]
            put_strip(hv, at, strip)
            put_strip(hf, at, coef_strip(strip))
    own = {HALO + k: k for k in range(HALO)} | {2 * HALO + k: ROWS - HALO + k for k in range(HALO)}
    moved = set()

    def value_of(e):
        return line_of(v, own[e]) if e in own and e not in moved else line_of(hv, e)

    def coef_of(e):
        return line_of(f, own[e]) if e in own else line_of(hf, e)

    def chain(first, before, last_after):
        value = value_of(first)
        here = coef_of(first) * value
        sofar = opened(value, here, before)
        for e in range(first, first + HALO):
            if e == first + HALO - 1 and last_after is not None:
                put_line(hv, e, sofar + last_after)
            else:
                value = value_of(e + 1)
                after = coef_of(e + 1) * value
                put_line(hv, e, sofar + after)
                if e < first + HALO - 1:
                    sofar = opened(value, after, here)
                here = after
            moved.add(e)

    for sweep in range(SWEEPS):
        chain(sweep + 1, coef_of(sweep) * value_of(sweep), line_of(kept, sweep))
        chain(3 * HALO - 1 - sweep, line_of(kept, HALO + sweep), None)
    sums[...] = sums_in[...]
    eye = (iota((PLANES, COLS), 0) == iota((PLANES, COLS), 1)).astype(BF16)
    for k in range(2 * HALO):
        i = k if k < HALO else ROWS - 2 * HALO + k
        put_plain(plain, k, line_of(hv, HALO + k))
        high, p, q = line_sums(plain[pl.ds(k * WIDE, COLS), :], weight_of(weights[...], i))
        sums[pl.ds(i, 1), :] = p
        sums[pl.ds(ROWS + i, 1), :] = q
        xe[pl.ds(k, PLANES, stride=2 * HALO), :] = nt(eye, high)
    sums[...] = jnp.transpose(sums[...])
    owners = send_ref.shape[0]
    each = LAYER // owners
    for c in range(3):
        for e in range(each):
            send_ref[:, c * each + e, :] = sums[pl.ds(c * LAYER + e, owners, stride=each), :]
    send_ref[:, 3 * each :, :] = jnp.zeros((owners, 8 - 3 * each, COLS), F32)


def final_kernel(got_ref, part, xe, out_ref, wall_ref):
    tiles = part[...].reshape(PLANES, ROWS // 8, 8, COLS)
    ends = xe[...].reshape(PLANES, 8, COLS)
    near = iota((PLANES, 8, COLS), 1) < HALO
    head = jnp.where(near, ends, tiles[:, 0])
    tail = jnp.where(near, tiles[:, 3], ends)
    out_ref[...] = jnp.concatenate([head, tiles[:, 1], tiles[:, 2], tail], axis=1).astype(BF16)
    owners = got_ref.shape[0]
    each = LAYER // owners
    own = [pltpu.roll(got_ref[d], COLS - 2 * ROWS, 1) for d in range(owners)]
    total = own[0]
    for d in range(1, owners):
        total = total + own[d]
    rest = total
    acc = jnp.zeros_like(total)
    moment = jnp.zeros_like(total)
    for d in range(owners):
        acc = acc + got_ref[d] * rest
        moment = moment + got_ref[d]
        rest = rest - own[d]
    acc = acc - pltpu.roll(moment, COLS - ROWS, 1)
    value = (acc / total) / total * math.sqrt(COLS * owners)
    for c in range(3):
        wall_ref[c] = value[c * each : (c + 1) * each, :ROWS]


def shaped(*shape):
    return jax.ShapeDtypeStruct(shape, F32)


def lines(count):
    return pltpu.VMEM((count * WIDE, COLS), F32)


def body(adjoint_in, coef, spacing):
    wraps, owners = lax.axis_size("wrap"), lax.axis_size("normal")
    everything = jnp.concatenate([adjoint_in.reshape(PLANES * ROWS, COLS).astype(F32), coef, spacing], axis=0)
    strip, square = shaped(ROWS, HALO, COLS), shaped(COLS, COLS)
    own_rows = shaped(ROWS * WIDE, COLS)
    to_cross, to_twin = call(strip_kernel, 1, [strip, strip], [], 1_000)(everything)
    to_twin = call(pass_kernel, 1, strip, [], 1_000)(to_twin)
    cross = lax.ppermute(to_cross, "normal", [(k, k + 1 if k % 2 else k - 1) for k in range(1, owners - 1)])
    cross = call(pass_kernel, 1, strip, [], 1_000)(cross)
    twin = lax.ppermute(to_twin, "normal", [(k, k ^ 1) for k in range(owners)])
    v, f, weights, sums = call(
        setup_kernel, 2, [own_rows, own_rows, square, square], [pltpu.VMEM((WIDE, COLS), F32)], 1_000
    )(everything, to_twin)
    top, bottom = call(rows_kernel, 2, [shaped(MAIN, COLS)] * 2, [], 1_000)(everything, sums)
    strips, top, bottom = call(corner_kernel, 4, [shaped(ROWS, 8, COLS), shaped(MSG, COLS), shaped(MSG, COLS)], [], 1_000)(
        cross, twin, top, bottom
    )
    above = lax.ppermute(bottom, "wrap", [(k, (k + 1) % wraps) for k in range(wraps)])
    below = lax.ppermute(top, "wrap", [((k + 1) % wraps, k) for k in range(wraps)])
    v, f, kept, part, sums = call(
        inner_kernel,
        5,
        [own_rows, own_rows, shaped(2 * HALO * WIDE, COLS), shaped(PLANES * ROWS, COLS), square],
        [],
        20_000_000_000,
        {0: 0, 1: 1},
    )(v, f, strips, weights, sums)
    ends, sums = call(
        outer_kernel,
        7,
        [shaped(PLANES * 2 * HALO, COLS), shaped(owners, 8, COLS)],
        [lines(4 * HALO), lines(4 * HALO), pltpu.VMEM((WIDE, COLS), F32), lines(2 * HALO), pltpu.VMEM((COLS, COLS), F32)],
        1_000,
    )(above, below, v, f, kept, sums, weights)
    got = lax.all_to_all(sums, "normal", 0, 0, tiled=True)
    adjoint_out, wall_sens = call(
        final_kernel,
        3,
        [jax.ShapeDtypeStruct((PLANES, ROWS, COLS), BF16), shaped(3, LAYER // owners, ROWS)],
        [],
        1_000,
    )(got, part, ends)
    return adjoint_out.reshape(3, LAYER, ROWS, COLS), wall_sens


def solution(mesh):
    placed = (P(None, None, "wrap", "normal"), P("wrap", "normal"), P("wrap", "normal"))
    return jax.shard_map(
        body,
        mesh=mesh,
        in_specs=placed,
        out_specs=(P(None, None, "wrap", "normal"), P(None, "normal", "wrap")),
        check_vma=False,
    )
```

```python
import math

import jax
import jax.numpy as jnp
from jax import lax
from jax.experimental import pallas as pl
from jax.experimental.pallas import tpu as pltpu
from jax.sharding import PartitionSpec as P

SWEEPS = 4
HALO = 4
PLANES = 96
LAYER = 32
ROWS = 32
COLS = 128
WIDE = COLS + 2 * HALO
STEPS = WIDE // 8
STRIP_AT = WIDE - 7 * 8 - 1
COEFS = HALO * PLANES
MAIN = COEFS + 8
MSG = MAIN + 8 * HALO
F32 = jnp.float32
BF16 = jnp.bfloat16
COEF_AT = PLANES * ROWS
SPACING_AT = COEF_AT + ROWS
ALL = SPACING_AT + ROWS
PARTS = 2
VMEM = pl.BlockSpec(memory_space=pltpu.VMEM)
HBM = pl.BlockSpec(memory_space=pltpu.HBM)


def nt(a, b):
    return lax.dot_general(a, b, (((1,), (1,)), ((), ())), preferred_element_type=F32)


def iota(shape, dim):
    return lax.broadcasted_iota(jnp.int32, shape, dim)


def call(kernel, ins, outs, scratch, cost, aliases=None):
    single = not isinstance(outs, (list, tuple))
    return pl.pallas_call(
        kernel,
        in_specs=ins if isinstance(ins, list) else [VMEM] * ins,
        out_shape=outs,
        out_specs=VMEM if single else [VMEM] * len(outs),
        scratch_shapes=scratch,
        input_output_aliases=aliases or {},
        compiler_params=pltpu.CompilerParams(vmem_limit_bytes=24 * 1024 * 1024),
        cost_estimate=pl.CostEstimate(flops=cost, bytes_accessed=1_000, transcendentals=0),
    )


def ring(line):
    return 17 * (line & 7) + (line >> 3)


def line_of(ref, r):
    return ref[pl.ds(pl.multiple_of(r * WIDE, 8), WIDE), :].reshape(STEPS, 8, COLS)


def put_line(ref, r, value):
    ref[pl.ds(pl.multiple_of(r * WIDE, 8), WIDE), :] = value.reshape(WIDE, COLS)


def put_plain(ref, r, value):
    for q in range(STEPS):
        ref[pl.ds(r * WIDE + q, 8, stride=STEPS), :] = value[q]


def put_strip(ref, r, strip):
    ref[pl.ds(r * WIDE + STRIP_AT, 8, stride=8), :] = strip


def opened(value, here, before):
    first = pltpu.roll(here[STEPS - 1], 1, 0)[None]
    last = pltpu.roll(here[0], 7, 0)[None]
    beside = jnp.concatenate([first, here[:-1]], axis=0) + jnp.concatenate([here[1:], last], axis=0)
    return (value - 4.0 * here) + (beside + before)


def selector():
    shape = (WIDE, COLS)
    return (ring(iota(shape, 0)) == iota(shape, 1)).astype(BF16)


def to_lanes(select, planes):
    pad = jnp.zeros((COLS - PLANES, COLS), BF16)
    return nt(select, jnp.concatenate([planes.astype(BF16), pad], axis=0))


def coef_strip(strip):
    return jnp.broadcast_to(strip[:, PLANES : PLANES + 1], (8, COLS))


def masked_ring(coef, scratch):
    rows = coef.shape[0]
    coef_t = jnp.transpose(jnp.concatenate([coef, jnp.zeros((COLS - rows, COLS), F32)], axis=0))
    place, last = lax.axis_index("normal"), lax.axis_size("normal") - 1
    col = iota((COLS, COLS), 0)
    outer = ((col == 0) & (place == 0)) | ((col == COLS - 1) & (place == last))
    scratch[pl.ds(0, COLS), :] = jnp.where(outer, 0.0, coef_t)
    scratch[pl.ds(COLS, 8), :] = jnp.zeros((8, COLS), F32)
    return jnp.concatenate([scratch[pl.ds(q, 8, stride=STEPS), :] for q in range(STEPS)], axis=0)


def line_sums(value, weight):
    high = value.astype(BF16)
    low = (value - high.astype(F32)).astype(BF16)
    both = lax.dot_general(
        jnp.concatenate([weight, weight], axis=1),
        jnp.concatenate([high, low], axis=0),
        (((1,), (0,)), ((), ())),
        preferred_element_type=F32,
    )
    return high, both[0:1] + both[2:3], both[1:2] + both[3:4]


def weight_of(weights, i):
    place = iota((16, COLS), 0)
    rows = [jnp.broadcast_to(weights[k * ROWS + i : k * ROWS + i + 1], (16, COLS)) for k in range(4)]
    rest = jnp.where(place == 2, rows[2], jnp.where(place == 3, rows[3], 0.0))
    return jnp.where(place == 0, rows[0], jnp.where(place == 1, rows[1], rest)).astype(BF16)


def split(value):
    high = value.astype(BF16).astype(F32)
    return high, value - high


def rows_kernel(all_ref, after_twin, top_ref, bottom_ref):
    zero = jnp.zeros((HALO, COLS), F32)
    for ref, at in ((top_ref, 0), (bottom_ref, ROWS - HALO)):
        for k in range(HALO):
            ref[pl.ds(k * PLANES, PLANES), :] = all_ref[pl.ds(at + k, PLANES, stride=ROWS), :]
        ref[pl.ds(COEFS, 8), :] = jnp.concatenate([all_ref[pl.ds(COEF_AT + at, HALO), :], zero], axis=0)


def strip_kernel(x_hbm, coef_hbm, spacing_hbm, all_ref, cross_ref, twin_ref, x_ref, sems):
    some = PLANES // PARTS
    copies = [
        pltpu.make_async_copy(coef_hbm, all_ref.at[pl.ds(COEF_AT, ROWS)], sems.at[PARTS]),
        pltpu.make_async_copy(spacing_hbm, all_ref.at[pl.ds(SPACING_AT, ROWS)], sems.at[PARTS + 1]),
    ]
    for k in range(PARTS):
        piece = pl.ds(k * some, some)
        copies.append(pltpu.make_async_copy(x_hbm.at[piece], x_ref.at[piece], sems.at[k]))
    for copy in copies[2:] + copies[:2]:
        copy.start()
    for k in range(PARTS):
        copies[k + 2].wait()
        piece = x_ref[pl.ds(k * some, some)].astype(F32)
        all_ref[pl.ds(k * some * ROWS, some * ROWS), :] = piece.reshape(some * ROWS, COLS)
    copies[0].wait()
    copies[1].wait()
    row, col = iota((2 * HALO, COLS), 0), iota((2 * HALO, COLS), 1)
    pick = (col == jnp.where(row < HALO, row, COLS - 2 * HALO + row)).astype(BF16)
    even = lax.axis_index("normal") % 2 == 0
    coef = all_ref[pl.ds(COEF_AT, ROWS), :]
    coef_t = jnp.transpose(jnp.concatenate([coef, jnp.zeros((COLS - ROWS, COLS), F32)], axis=0))
    ends = jnp.concatenate([coef_t[:HALO], coef_t[COLS - HALO :]], axis=0)
    pad = jnp.zeros((COLS - PLANES, COLS), BF16)
    for i in range(ROWS):
        planes = all_ref[pl.ds(i, PLANES, stride=ROWS), :]
        strip = nt(pick, jnp.concatenate([planes.astype(BF16), pad], axis=0))
        strip = jnp.where(col < PLANES, strip, jnp.broadcast_to(ends[:, i : i + 1], (2 * HALO, COLS)))
        cross_ref[i] = jnp.where(even, strip[:HALO], strip[HALO:])
        twin_ref[i] = jnp.where(even, strip[HALO:], strip[:HALO])


def pass_kernel(ref, out_ref):
    out_ref[...] = ref[...]


def corner_kernel(cross, twin, top, bottom, strips_ref, top_ref, bottom_ref):
    even = lax.axis_index("normal") % 2 == 0
    right = jnp.where(even, twin[...], cross[...])
    left = jnp.where(even, cross[...], twin[...])
    strips = jnp.concatenate([right, left], axis=1)
    strips_ref[...] = strips
    top_ref[pl.ds(0, MAIN), :] = top[...]
    bottom_ref[pl.ds(0, MAIN), :] = bottom[...]
    for r in range(HALO):
        top_ref[pl.ds(MAIN + 8 * r, 8), :] = strips[r]
        bottom_ref[pl.ds(MAIN + 8 * r, 8), :] = strips[ROWS - HALO + r]


def setup_kernel(all_ref, after_corner, v, f, weights, sums, ct):
    select = selector()
    ring_coef = masked_ring(all_ref[pl.ds(COEF_AT, ROWS), :], ct)
    for r in range(ROWS):
        v[pl.ds(r * WIDE, WIDE), :] = to_lanes(select, all_ref[pl.ds(r, PLANES, stride=ROWS), :])
        f[pl.ds(r * WIDE, WIDE), :] = jnp.broadcast_to(ring_coef[:, r : r + 1], (WIDE, COLS))
    spacing = all_ref[pl.ds(SPACING_AT, ROWS), :]
    earlier = (iota((COLS, COLS), 0) < iota((COLS, COLS), 1)).astype(F32)
    before = lax.dot_general(
        spacing, earlier, (((1,), (0,)), ((), ())), preferred_element_type=F32, precision=lax.Precision.HIGHEST
    )
    s_high, s_low = split(spacing)
    q_high, q_low = split(before * spacing)
    weights[...] = jnp.concatenate([s_high, q_high, s_low, q_low], axis=0)
    total = jnp.broadcast_to(jnp.sum(spacing, axis=1, keepdims=True), (ROWS, COLS))
    empty = jnp.zeros((ROWS, COLS), F32)
    sums[...] = jnp.concatenate([empty, empty, total, empty], axis=0)


def inner_kernel(v_in, f_in, strips, weights, sums_in, v, f, kept, part, sums):
    for r in range(ROWS):
        put_strip(v, r, strips[r])
        put_strip(f, r, coef_strip(strips[r]))

    for sweep in range(SWEEPS):
        put = put_line if sweep < SWEEPS - 1 else put_plain
        low, high = sweep + 1, ROWS - 2 - sweep

        def step(r, held):
            sofar, here = held
            value = line_of(v, r + 1)
            after = line_of(f, r + 1) * value
            put(v, r, sofar + after)
            return opened(value, after, here), after

        value = line_of(v, low)
        here = line_of(f, low) * value
        put_line(kept, sweep, here)
        held = (opened(value, here, line_of(f, low - 1) * line_of(v, low - 1)), here)
        held = lax.fori_loop(low, high, step, held, unroll=4)
        put_line(kept, HALO + sweep, held[1])
        put(v, high, held[0] + line_of(f, high + 1) * line_of(v, high + 1))

    sums[...] = sums_in[...]
    eye = (iota((PLANES, COLS), 0) == iota((PLANES, COLS), 1)).astype(BF16)
    for i in range(HALO, ROWS - HALO):
        high, p, q = line_sums(v[pl.ds(i * WIDE, COLS), :], weight_of(weights[...], i))
        sums[pl.ds(i, 1), :] = p
        sums[pl.ds(ROWS + i, 1), :] = q
        part[pl.ds(i, PLANES, stride=ROWS), :] = nt(eye, high)


def outer_kernel(above, below, v, f, kept, sums_in, weights, xe, send_ref, hv, hf, ct, plain, sums):
    select = selector()
    ring_coef = masked_ring(jnp.concatenate([above[pl.ds(COEFS, HALO), :], below[pl.ds(COEFS, HALO), :]], axis=0), ct)
    for k in range(HALO):
        for message, at, c in ((above, k, k), (below, 3 * HALO + k, HALO + k)):
            hv[pl.ds(at * WIDE, WIDE), :] = to_lanes(select, message[pl.ds(k * PLANES, PLANES), :])
            hf[pl.ds(at * WIDE, WIDE), :] = jnp.broadcast_to(ring_coef[:, c : c + 1], (WIDE, COLS))
            strip = message[pl.ds(MAIN + 8 * k, 8), :]
            put_strip(hv, at, strip)
            put_strip(hf, at, coef_strip(strip))
    own = {HALO + k: k for k in range(HALO)} | {2 * HALO + k: ROWS - HALO + k for k in range(HALO)}
    moved = set()

    def value_of(e):
        return line_of(v, own[e]) if e in own and e not in moved else line_of(hv, e)

    def coef_of(e):
        return line_of(f, own[e]) if e in own else line_of(hf, e)

    def chain(first, before, last_after):
        value = value_of(first)
        here = coef_of(first) * value
        sofar = opened(value, here, before)
        for e in range(first, first + HALO):
            if e == first + HALO - 1 and last_after is not None:
                put_line(hv, e, sofar + last_after)
            else:
                value = value_of(e + 1)
                after = coef_of(e + 1) * value
                put_line(hv, e, sofar + after)
                if e < first + HALO - 1:
                    sofar = opened(value, after, here)
                here = after
            moved.add(e)

    for sweep in range(SWEEPS):
        chain(sweep + 1, coef_of(sweep) * value_of(sweep), line_of(kept, sweep))
        chain(3 * HALO - 1 - sweep, line_of(kept, HALO + sweep), None)
    sums[...] = sums_in[...]
    eye = (iota((PLANES, COLS), 0) == iota((PLANES, COLS), 1)).astype(BF16)
    for k in range(2 * HALO):
        i = k if k < HALO else ROWS - 2 * HALO + k
        put_plain(plain, k, line_of(hv, HALO + k))
        high, p, q = line_sums(plain[pl.ds(k * WIDE, COLS), :], weight_of(weights[...], i))
        sums[pl.ds(i, 1), :] = p
        sums[pl.ds(ROWS + i, 1), :] = q
        xe[pl.ds(k, PLANES, stride=2 * HALO), :] = nt(eye, high)
    sums[...] = jnp.transpose(sums[...])
    owners = send_ref.shape[0]
    each = LAYER // owners
    for c in range(3):
        for e in range(each):
            send_ref[:, c * each + e, :] = sums[pl.ds(c * LAYER + e, owners, stride=each), :]
    send_ref[:, 3 * each :, :] = jnp.zeros((owners, 8 - 3 * each, COLS), F32)


def final_kernel(got_ref, part, xe, out_ref, wall_ref):
    tiles = part[...].reshape(PLANES, ROWS // 8, 8, COLS)
    ends = xe[...].reshape(PLANES, 8, COLS)
    near = iota((PLANES, 8, COLS), 1) < HALO
    head = jnp.where(near, ends, tiles[:, 0])
    tail = jnp.where(near, tiles[:, 3], ends)
    out_ref[...] = jnp.concatenate([head, tiles[:, 1], tiles[:, 2], tail], axis=1).astype(BF16)
    owners = got_ref.shape[0]
    each = LAYER // owners
    own = [pltpu.roll(got_ref[d], COLS - 2 * ROWS, 1) for d in range(owners)]
    total = own[0]
    for d in range(1, owners):
        total = total + own[d]
    rest = total
    acc = jnp.zeros_like(total)
    moment = jnp.zeros_like(total)
    for d in range(owners):
        acc = acc + got_ref[d] * rest
        moment = moment + got_ref[d]
        rest = rest - own[d]
    acc = acc - pltpu.roll(moment, COLS - ROWS, 1)
    value = (acc / total) / total * math.sqrt(COLS * owners)
    for c in range(3):
        wall_ref[c] = value[c * each : (c + 1) * each, :ROWS]


def shaped(*shape):
    return jax.ShapeDtypeStruct(shape, F32)


def lines(count):
    return pltpu.VMEM((count * WIDE, COLS), F32)


def body(adjoint_in, coef, spacing):
    wraps, owners = lax.axis_size("wrap"), lax.axis_size("normal")
    strip, square = shaped(ROWS, HALO, COLS), shaped(COLS, COLS)
    own_rows = shaped(ROWS * WIDE, COLS)
    x = adjoint_in.reshape(PLANES, ROWS, COLS)
    everything, to_cross, to_twin = call(
        strip_kernel,
        [HBM] * 3,
        [shaped(ALL, COLS), strip, strip],
        [pltpu.VMEM((PLANES, ROWS, COLS), BF16), pltpu.SemaphoreType.DMA((PARTS + 2,))],
        1_000,
    )(*[pltpu.with_memory_space_constraint(a, pltpu.HBM) for a in (x, coef, spacing)])
    to_twin = call(pass_kernel, 1, strip, [], 1_000)(to_twin)
    cross = lax.ppermute(to_cross, "normal", [(k, k + 1 if k % 2 else k - 1) for k in range(1, owners - 1)])
    cross = call(pass_kernel, 1, strip, [], 1_000)(cross)
    twin = lax.ppermute(to_twin, "normal", [(k, k ^ 1) for k in range(owners)])
    top, bottom = call(rows_kernel, 2, [shaped(MAIN, COLS)] * 2, [], 1_000)(everything, to_twin)
    strips, top, bottom = call(corner_kernel, 4, [shaped(ROWS, 8, COLS), shaped(MSG, COLS), shaped(MSG, COLS)], [], 1_000)(
        cross, twin, top, bottom
    )
    v, f, weights, sums = call(
        setup_kernel, 2, [own_rows, own_rows, square, square], [pltpu.VMEM((WIDE, COLS), F32)], 1_000
    )(everything, strips)
    above = lax.ppermute(bottom, "wrap", [(k, (k + 1) % wraps) for k in range(wraps)])
    below = lax.ppermute(top, "wrap", [((k + 1) % wraps, k) for k in range(wraps)])
    v, f, kept, part, sums = call(
        inner_kernel,
        5,
        [own_rows, own_rows, shaped(2 * HALO * WIDE, COLS), shaped(PLANES * ROWS, COLS), square],
        [],
        20_000_000_000,
        {0: 0, 1: 1},
    )(v, f, strips, weights, sums)
    ends, sums = call(
        outer_kernel,
        7,
        [shaped(PLANES * 2 * HALO, COLS), shaped(owners, 8, COLS)],
        [lines(4 * HALO), lines(4 * HALO), pltpu.VMEM((WIDE, COLS), F32), lines(2 * HALO), pltpu.VMEM((COLS, COLS), F32)],
        1_000,
    )(above, below, v, f, kept, sums, weights)
    got = lax.all_to_all(sums, "normal", 0, 0, tiled=True)
    adjoint_out, wall_sens = call(
        final_kernel,
        3,
        [jax.ShapeDtypeStruct((PLANES, ROWS, COLS), BF16), shaped(3, LAYER // owners, ROWS)],
        [],
        1_000,
    )(got, part, ends)
    return adjoint_out.reshape(3, LAYER, ROWS, COLS), wall_sens


def solution(mesh):
    placed = (P(None, None, "wrap", "normal"), P("wrap", "normal"), P("wrap", "normal"))
    return jax.shard_map(
        body,
        mesh=mesh,
        in_specs=placed,
        out_specs=(P(None, None, "wrap", "normal"), P(None, "normal", "wrap")),
        check_vma=False,
    )
```

```python
import math

import jax
import jax.numpy as jnp
from jax import lax
from jax.experimental import pallas as pl
from jax.experimental.pallas import tpu as pltpu
from jax.sharding import PartitionSpec as P

SWEEPS = 4
HALO = 4
PLANES = 96
LAYER = 32
ROWS = 32
COLS = 128
WIDE = COLS + 2 * HALO
STEPS = WIDE // 8
STRIP_AT = WIDE - 7 * 8 - 1
COEFS = HALO * PLANES
MAIN = COEFS + 8
MSG = MAIN + 8 * HALO
SPARE = 3 * 8
F32 = jnp.float32
BF16 = jnp.bfloat16
COEF_AT = PLANES * ROWS
SPACING_AT = COEF_AT + ROWS
ALL = SPACING_AT + ROWS
PARTS = 2
VMEM = pl.BlockSpec(memory_space=pltpu.VMEM)
HBM = pl.BlockSpec(memory_space=pltpu.HBM)


def nt(a, b):
    return lax.dot_general(a, b, (((1,), (1,)), ((), ())), preferred_element_type=F32)


def iota(shape, dim):
    return lax.broadcasted_iota(jnp.int32, shape, dim)


def call(kernel, ins, outs, scratch, cost, aliases=None):
    single = not isinstance(outs, (list, tuple))
    return pl.pallas_call(
        kernel,
        in_specs=ins if isinstance(ins, list) else [VMEM] * ins,
        out_shape=outs,
        out_specs=VMEM if single else [VMEM] * len(outs),
        scratch_shapes=scratch,
        input_output_aliases=aliases or {},
        compiler_params=pltpu.CompilerParams(vmem_limit_bytes=24 * 1024 * 1024),
        cost_estimate=pl.CostEstimate(flops=cost, bytes_accessed=1_000, transcendentals=0),
    )


def ring(line):
    return 17 * (line & 7) + (line >> 3)


def line_of(ref, r):
    return ref[pl.ds(pl.multiple_of(r * WIDE, 8), WIDE), :].reshape(STEPS, 8, COLS)


def put_line(ref, r, value):
    ref[pl.ds(pl.multiple_of(r * WIDE, 8), WIDE), :] = value.reshape(WIDE, COLS)


def put_plain(ref, r, value):
    for q in range(STEPS):
        ref[pl.ds(r * WIDE + q, 8, stride=STEPS), :] = value[q]


def put_strip(ref, r, strip):
    ref[pl.ds(r * WIDE + STRIP_AT, 8, stride=8), :] = strip


def opened(value, here, before):
    first = pltpu.roll(here[STEPS - 1], 1, 0)[None]
    last = pltpu.roll(here[0], 7, 0)[None]
    beside = jnp.concatenate([first, here[:-1]], axis=0) + jnp.concatenate([here[1:], last], axis=0)
    return (value - 4.0 * here) + (beside + before)


def selector():
    shape = (WIDE, COLS)
    return (ring(iota(shape, 0)) == iota(shape, 1)).astype(BF16)


def to_lanes(select, planes):
    pad = jnp.zeros((COLS - PLANES, COLS), BF16)
    return nt(select, jnp.concatenate([planes.astype(BF16), pad], axis=0))


def coef_strip(strip):
    return jnp.broadcast_to(strip[:, PLANES : PLANES + 1], (8, COLS))


def masked_ring(coef, scratch):
    rows = coef.shape[0]
    coef_t = jnp.transpose(jnp.concatenate([coef, jnp.zeros((COLS - rows, COLS), F32)], axis=0))
    place, last = lax.axis_index("normal"), lax.axis_size("normal") - 1
    col = iota((COLS, COLS), 0)
    outer = ((col == 0) & (place == 0)) | ((col == COLS - 1) & (place == last))
    scratch[pl.ds(0, COLS), :] = jnp.where(outer, 0.0, coef_t)
    scratch[pl.ds(COLS, 8), :] = jnp.zeros((8, COLS), F32)
    return jnp.concatenate([scratch[pl.ds(q, 8, stride=STEPS), :] for q in range(STEPS)], axis=0)


def line_sums(value, weight):
    high = value.astype(BF16)
    low = (value - high.astype(F32)).astype(BF16)
    both = lax.dot_general(
        jnp.concatenate([weight, weight], axis=1),
        jnp.concatenate([high, low], axis=0),
        (((1,), (0,)), ((), ())),
        preferred_element_type=F32,
    )
    return high, both[0:1] + both[2:3], both[1:2] + both[3:4]


def weight_of(weights, i):
    place = iota((16, COLS), 0)
    rows = [jnp.broadcast_to(weights[k * ROWS + i : k * ROWS + i + 1], (16, COLS)) for k in range(4)]
    rest = jnp.where(place == 2, rows[2], jnp.where(place == 3, rows[3], 0.0))
    return jnp.where(place == 0, rows[0], jnp.where(place == 1, rows[1], rest)).astype(BF16)


def split(value):
    high = value.astype(BF16).astype(F32)
    return high, value - high


def rows_kernel(all_ref, after_twin, top_ref, bottom_ref):
    zero = jnp.zeros((HALO, COLS), F32)
    for ref, at in ((top_ref, 0), (bottom_ref, ROWS - HALO)):
        for k in range(HALO):
            ref[pl.ds(k * PLANES, PLANES), :] = all_ref[pl.ds(at + k, PLANES, stride=ROWS), :]
        ref[pl.ds(COEFS, 8), :] = jnp.concatenate([all_ref[pl.ds(COEF_AT + at, HALO), :], zero], axis=0)


def strip_kernel(x_hbm, coef_hbm, spacing_hbm, all_ref, cross_ref, twin_ref, x_ref, sems):
    some = PLANES // PARTS
    copies = [
        pltpu.make_async_copy(coef_hbm, all_ref.at[pl.ds(COEF_AT, ROWS)], sems.at[PARTS]),
        pltpu.make_async_copy(spacing_hbm, all_ref.at[pl.ds(SPACING_AT, ROWS)], sems.at[PARTS + 1]),
    ]
    for k in range(PARTS):
        piece = pl.ds(k * some, some)
        copies.append(pltpu.make_async_copy(x_hbm.at[piece], x_ref.at[piece], sems.at[k]))
    for copy in copies[2:] + copies[:2]:
        copy.start()
    for k in range(PARTS):
        copies[k + 2].wait()
        piece = x_ref[pl.ds(k * some, some)].astype(F32)
        all_ref[pl.ds(k * some * ROWS, some * ROWS), :] = piece.reshape(some * ROWS, COLS)
    copies[0].wait()
    copies[1].wait()
    row, col = iota((2 * HALO, COLS), 0), iota((2 * HALO, COLS), 1)
    pick = (col == jnp.where(row < HALO, row, COLS - 2 * HALO + row)).astype(BF16)
    even = lax.axis_index("normal") % 2 == 0
    coef = all_ref[pl.ds(COEF_AT, ROWS), :]
    coef_t = jnp.transpose(jnp.concatenate([coef, jnp.zeros((COLS - ROWS, COLS), F32)], axis=0))
    ends = jnp.concatenate([coef_t[:HALO], coef_t[COLS - HALO :]], axis=0)
    pad = jnp.zeros((COLS - PLANES, COLS), BF16)
    for i in range(ROWS):
        planes = all_ref[pl.ds(i, PLANES, stride=ROWS), :]
        strip = nt(pick, jnp.concatenate([planes.astype(BF16), pad], axis=0))
        strip = jnp.where(col < PLANES, strip, jnp.broadcast_to(ends[:, i : i + 1], (2 * HALO, COLS)))
        cross_ref[i] = jnp.where(even, strip[:HALO], strip[HALO:])
        twin_ref[i] = jnp.where(even, strip[HALO:], strip[:HALO])


def pass_kernel(ref, out_ref):
    out_ref[...] = ref[...]


def corner_kernel(cross, twin, top, bottom, strips_ref, top_ref, bottom_ref):
    even = lax.axis_index("normal") % 2 == 0
    right = jnp.where(even, twin[...], cross[...])
    left = jnp.where(even, cross[...], twin[...])
    strips = jnp.concatenate([right, left], axis=1)
    strips_ref[...] = strips
    top_ref[pl.ds(0, MAIN), :] = top[...]
    bottom_ref[pl.ds(0, MAIN), :] = bottom[...]
    for r in range(HALO):
        top_ref[pl.ds(MAIN + 8 * r, 8), :] = strips[r]
        bottom_ref[pl.ds(MAIN + 8 * r, 8), :] = strips[ROWS - HALO + r]


def setup_kernel(all_ref, after_corner, v, f, weights, sums, ct):
    select = selector()
    ring_coef = masked_ring(all_ref[pl.ds(COEF_AT, ROWS), :], ct)
    for r in range(ROWS):
        v[pl.ds(r * WIDE, WIDE), :] = to_lanes(select, all_ref[pl.ds(r, PLANES, stride=ROWS), :])
        f[pl.ds(r * WIDE, WIDE), :] = jnp.broadcast_to(ring_coef[:, r : r + 1], (WIDE, COLS))
    spacing = all_ref[pl.ds(SPACING_AT, ROWS), :]
    earlier = (iota((COLS, COLS), 0) < iota((COLS, COLS), 1)).astype(F32)
    before = lax.dot_general(
        spacing, earlier, (((1,), (0,)), ((), ())), preferred_element_type=F32, precision=lax.Precision.HIGHEST
    )
    s_high, s_low = split(spacing)
    q_high, q_low = split(before * spacing)
    weights[...] = jnp.concatenate([s_high, q_high, s_low, q_low], axis=0)
    total = jnp.broadcast_to(jnp.sum(spacing, axis=1, keepdims=True), (ROWS, COLS))
    empty = jnp.zeros((ROWS, COLS), F32)
    sums[...] = jnp.concatenate([empty, empty, total, empty], axis=0)


def inner_kernel(v_in, f_in, strips, weights, sums_in, v, f, kept, part, sums):
    for r in range(ROWS):
        put_strip(v, r, strips[r])
        put_strip(f, r, coef_strip(strips[r]))

    for sweep in range(SWEEPS):
        put = put_line if sweep < SWEEPS - 1 else put_plain
        low, high = sweep + 1, ROWS - 2 - sweep

        def step(r, held):
            sofar, here = held
            value = line_of(v, r + 1)
            after = line_of(f, r + 1) * value
            put(v, r, sofar + after)
            return opened(value, after, here), after

        value = line_of(v, low)
        here = line_of(f, low) * value
        put_line(kept, sweep, here)
        held = (opened(value, here, line_of(f, low - 1) * line_of(v, low - 1)), here)
        held = lax.fori_loop(low, high, step, held, unroll=4)
        put_line(kept, HALO + sweep, held[1])
        put(v, high, held[0] + line_of(f, high + 1) * line_of(v, high + 1))

    sums[...] = sums_in[...]
    eye = (iota((PLANES, COLS), 0) == iota((PLANES, COLS), 1)).astype(BF16)
    for i in range(HALO, ROWS - HALO):
        high, p, q = line_sums(v[pl.ds(i * WIDE, COLS), :], weight_of(weights[...], i))
        sums[pl.ds(i, 1), :] = p
        sums[pl.ds(ROWS + i, 1), :] = q
        part[pl.ds(i, PLANES, stride=ROWS), :] = nt(eye, high)


def outer_kernel(above, below, v, f, kept, sums_in, weights, xe, send_ref, hv, hf, ct, plain, sums):
    select = selector()
    ring_coef = masked_ring(jnp.concatenate([above[pl.ds(COEFS, HALO), :], below[pl.ds(COEFS, HALO), :]], axis=0), ct)
    for k in range(HALO):
        for message, at, c in ((above, k, k), (below, 3 * HALO + k, HALO + k)):
            hv[pl.ds(at * WIDE, WIDE), :] = to_lanes(select, message[pl.ds(k * PLANES, PLANES), :])
            hf[pl.ds(at * WIDE, WIDE), :] = jnp.broadcast_to(ring_coef[:, c : c + 1], (WIDE, COLS))
            strip = message[pl.ds(MAIN + 8 * k, 8), :]
            put_strip(hv, at, strip)
            put_strip(hf, at, coef_strip(strip))
    own = {HALO + k: k for k in range(HALO)} | {2 * HALO + k: ROWS - HALO + k for k in range(HALO)}
    moved = set()

    def value_of(e):
        return line_of(v, own[e]) if e in own and e not in moved else line_of(hv, e)

    def coef_of(e):
        return line_of(f, own[e]) if e in own else line_of(hf, e)

    def chain(first, before, last_after):
        value = value_of(first)
        here = coef_of(first) * value
        sofar = opened(value, here, before)
        for e in range(first, first + HALO):
            if e == first + HALO - 1 and last_after is not None:
                put_line(hv, e, sofar + last_after)
            else:
                value = value_of(e + 1)
                after = coef_of(e + 1) * value
                put_line(hv, e, sofar + after)
                if e < first + HALO - 1:
                    sofar = opened(value, after, here)
                here = after
            moved.add(e)

    for sweep in range(SWEEPS):
        chain(sweep + 1, coef_of(sweep) * value_of(sweep), line_of(kept, sweep))
        chain(3 * HALO - 1 - sweep, line_of(kept, HALO + sweep), None)
    sums[...] = sums_in[...]
    eye = (iota((PLANES, COLS), 0) == iota((PLANES, COLS), 1)).astype(BF16)
    for k in range(2 * HALO):
        i = k if k < HALO else ROWS - 2 * HALO + k
        put_plain(plain, k, line_of(hv, HALO + k))
        high, p, q = line_sums(plain[pl.ds(k * WIDE, COLS), :], weight_of(weights[...], i))
        sums[pl.ds(i, 1), :] = p
        sums[pl.ds(ROWS + i, 1), :] = q
        xe[pl.ds(k, PLANES, stride=2 * HALO), :] = nt(eye, high)
    sums[...] = jnp.transpose(sums[...])
    owners = send_ref.shape[0]
    each = LAYER // owners
    for c in range(3):
        for e in range(each):
            send_ref[:, c * each + e, :] = sums[pl.ds(c * LAYER + e, owners, stride=each), :]
    send_ref[:, 3 * each :, :] = jnp.zeros((owners, 8 - 3 * each, COLS), F32)


def final_kernel(got_ref, part, xe, out_ref, wall_ref):
    tiles = part[pl.ds(0, PLANES * ROWS), :].reshape(PLANES, ROWS // 8, 8, COLS)
    ends = xe[pl.ds(0, PLANES * 8), :].reshape(PLANES, 8, COLS)
    near = iota((PLANES, 8, COLS), 1) < HALO
    head = jnp.where(near, ends, tiles[:, 0])
    tail = jnp.where(near, tiles[:, 3], ends)
    out_ref[...] = jnp.concatenate([head, tiles[:, 1], tiles[:, 2], tail], axis=1).astype(BF16)
    owners = got_ref.shape[0]
    each = LAYER // owners
    own = [pltpu.roll(got_ref[d], COLS - 2 * ROWS, 1) for d in range(owners)]
    total = own[0]
    for d in range(1, owners):
        total = total + own[d]
    rest = total
    acc = jnp.zeros_like(total)
    moment = jnp.zeros_like(total)
    for d in range(owners):
        acc = acc + got_ref[d] * rest
        moment = moment + got_ref[d]
        rest = rest - own[d]
    acc = acc - pltpu.roll(moment, COLS - ROWS, 1)
    value = (acc / total) / total * math.sqrt(COLS * owners)
    for c in range(3):
        wall_ref[c] = value[c * each : (c + 1) * each, :ROWS]


def shaped(*shape):
    return jax.ShapeDtypeStruct(shape, F32)


def lines(count):
    return pltpu.VMEM((count * WIDE + SPARE, COLS), F32)


def body(adjoint_in, coef, spacing):
    wraps, owners = lax.axis_size("wrap"), lax.axis_size("normal")
    strip, square = shaped(ROWS, HALO, COLS), shaped(COLS, COLS)
    own_rows = shaped(ROWS * WIDE + SPARE, COLS)
    x = adjoint_in.reshape(PLANES, ROWS, COLS)
    everything, to_cross, to_twin = call(
        strip_kernel,
        [HBM] * 3,
        [shaped(ALL, COLS), strip, strip],
        [pltpu.VMEM((PLANES, ROWS, COLS), BF16), pltpu.SemaphoreType.DMA((PARTS + 2,))],
        1_000,
    )(*[pltpu.with_memory_space_constraint(a, pltpu.HBM) for a in (x, coef, spacing)])
    to_twin = call(pass_kernel, 1, strip, [], 1_000)(to_twin)
    cross = lax.ppermute(to_cross, "normal", [(k, k + 1 if k % 2 else k - 1) for k in range(1, owners - 1)])
    cross = call(pass_kernel, 1, strip, [], 1_000)(cross)
    twin = lax.ppermute(to_twin, "normal", [(k, k ^ 1) for k in range(owners)])
    top, bottom = call(rows_kernel, 2, [shaped(MAIN, COLS)] * 2, [], 1_000)(everything, to_twin)
    strips, top, bottom = call(corner_kernel, 4, [shaped(ROWS, 8, COLS), shaped(MSG, COLS), shaped(MSG, COLS)], [], 1_000)(
        cross, twin, top, bottom
    )
    v, f, weights, sums = call(
        setup_kernel, 2, [own_rows, own_rows, square, square], [pltpu.VMEM((WIDE + SPARE, COLS), F32)], 1_000
    )(everything, strips)
    above = lax.ppermute(bottom, "wrap", [(k, (k + 1) % wraps) for k in range(wraps)])
    below = lax.ppermute(top, "wrap", [((k + 1) % wraps, k) for k in range(wraps)])
    v, f, kept, part, sums = call(
        inner_kernel,
        5,
        [own_rows, own_rows, shaped(2 * HALO * WIDE, COLS), shaped(PLANES * ROWS + ROWS, COLS), square],
        [],
        20_000_000_000,
        {0: 0, 1: 1},
    )(v, f, strips, weights, sums)
    ends, sums = call(
        outer_kernel,
        7,
        [shaped(PLANES * 2 * HALO + 2 * HALO, COLS), shaped(owners, 8, COLS)],
        [lines(4 * HALO), lines(4 * HALO), pltpu.VMEM((WIDE + SPARE, COLS), F32), lines(2 * HALO), pltpu.VMEM((COLS, COLS), F32)],
        1_000,
    )(above, below, v, f, kept, sums, weights)
    got = lax.all_to_all(sums, "normal", 0, 0, tiled=True)
    adjoint_out, wall_sens = call(
        final_kernel,
        3,
        [jax.ShapeDtypeStruct((PLANES, ROWS, COLS), BF16), shaped(3, LAYER // owners, ROWS)],
        [],
        1_000,
    )(got, part, ends)
    return adjoint_out.reshape(3, LAYER, ROWS, COLS), wall_sens


def solution(mesh):
    placed = (P(None, None, "wrap", "normal"), P("wrap", "normal"), P("wrap", "normal"))
    return jax.shard_map(
        body,
        mesh=mesh,
        in_specs=placed,
        out_specs=(P(None, None, "wrap", "normal"), P(None, "normal", "wrap")),
        check_vma=False,
    )
```

```python
import math

import jax
import jax.numpy as jnp
from jax import lax
from jax.experimental import pallas as pl
from jax.experimental.pallas import tpu as pltpu
from jax.sharding import PartitionSpec as P

SWEEPS = 4
HALO = 4
PLANES = 96
LAYER = 32
ROWS = 32
COLS = 128
WIDE = COLS + 2 * HALO
STEPS = WIDE // 8
STRIP_AT = WIDE - 7 * 8 - 1
COEFS = HALO * PLANES
MAIN = COEFS + 8
MSG = MAIN + 8 * (HALO - 1)
SPARE = 3 * 8
F32 = jnp.float32
BF16 = jnp.bfloat16
COEF_AT = PLANES * ROWS
SPACING_AT = COEF_AT + ROWS
ALL = SPACING_AT + ROWS
PARTS = 2
VMEM = pl.BlockSpec(memory_space=pltpu.VMEM)
HBM = pl.BlockSpec(memory_space=pltpu.HBM)


def nt(a, b):
    return lax.dot_general(a, b, (((1,), (1,)), ((), ())), preferred_element_type=F32)


def iota(shape, dim):
    return lax.broadcasted_iota(jnp.int32, shape, dim)


def call(kernel, ins, outs, scratch, cost, aliases=None):
    single = not isinstance(outs, (list, tuple))
    return pl.pallas_call(
        kernel,
        in_specs=ins if isinstance(ins, list) else [VMEM] * ins,
        out_shape=outs,
        out_specs=VMEM if single else [VMEM] * len(outs),
        scratch_shapes=scratch,
        input_output_aliases=aliases or {},
        compiler_params=pltpu.CompilerParams(vmem_limit_bytes=24 * 1024 * 1024),
        cost_estimate=pl.CostEstimate(flops=cost, bytes_accessed=1_000, transcendentals=0),
    )


def ring(line):
    return 17 * (line & 7) + (line >> 3)


def line_of(ref, r):
    return ref[pl.ds(pl.multiple_of(r * WIDE, 8), WIDE), :].reshape(STEPS, 8, COLS)


def put_line(ref, r, value):
    ref[pl.ds(pl.multiple_of(r * WIDE, 8), WIDE), :] = value.reshape(WIDE, COLS)


def put_plain(ref, r, value):
    for q in range(STEPS):
        ref[pl.ds(r * WIDE + q, 8, stride=STEPS), :] = value[q]


def put_strip(ref, r, strip):
    ref[pl.ds(r * WIDE + STRIP_AT, 8, stride=8), :] = strip


def opened(value, here, before):
    first = pltpu.roll(here[STEPS - 1], 1, 0)[None]
    last = pltpu.roll(here[0], 7, 0)[None]
    beside = jnp.concatenate([first, here[:-1]], axis=0) + jnp.concatenate([here[1:], last], axis=0)
    return (value - 4.0 * here) + (beside + before)


def selector():
    shape = (WIDE, COLS)
    return (ring(iota(shape, 0)) == iota(shape, 1)).astype(BF16)


def to_lanes(select, planes):
    pad = jnp.zeros((COLS - PLANES, COLS), BF16)
    return nt(select, jnp.concatenate([planes.astype(BF16), pad], axis=0))


def coef_strip(strip):
    return jnp.broadcast_to(strip[:, PLANES : PLANES + 1], (8, COLS))


def masked_ring(coef, scratch):
    rows = coef.shape[0]
    coef_t = jnp.transpose(jnp.concatenate([coef, jnp.zeros((COLS - rows, COLS), F32)], axis=0))
    place, last = lax.axis_index("normal"), lax.axis_size("normal") - 1
    col = iota((COLS, COLS), 0)
    outer = ((col == 0) & (place == 0)) | ((col == COLS - 1) & (place == last))
    scratch[pl.ds(0, COLS), :] = jnp.where(outer, 0.0, coef_t)
    scratch[pl.ds(COLS, 8), :] = jnp.zeros((8, COLS), F32)
    return jnp.concatenate([scratch[pl.ds(q, 8, stride=STEPS), :] for q in range(STEPS)], axis=0)


def line_sums(value, weight):
    high = value.astype(BF16)
    low = (value - high.astype(F32)).astype(BF16)
    both = lax.dot_general(
        jnp.concatenate([weight, weight], axis=1),
        jnp.concatenate([high, low], axis=0),
        (((1,), (0,)), ((), ())),
        preferred_element_type=F32,
    )
    return high, both[0:1] + both[2:3], both[1:2] + both[3:4]


def weight_of(weights, i):
    place = iota((16, COLS), 0)
    rows = [jnp.broadcast_to(weights[k * ROWS + i : k * ROWS + i + 1], (16, COLS)) for k in range(4)]
    rest = jnp.where(place == 2, rows[2], jnp.where(place == 3, rows[3], 0.0))
    return jnp.where(place == 0, rows[0], jnp.where(place == 1, rows[1], rest)).astype(BF16)


def split(value):
    high = value.astype(BF16).astype(F32)
    return high, value - high


def rows_kernel(all_ref, after_twin, top_ref, bottom_ref):
    zero = jnp.zeros((HALO, COLS), F32)
    for ref, at in ((top_ref, 0), (bottom_ref, ROWS - HALO)):
        for k in range(HALO):
            ref[pl.ds(k * PLANES, PLANES), :] = all_ref[pl.ds(at + k, PLANES, stride=ROWS), :]
        ref[pl.ds(COEFS, 8), :] = jnp.concatenate([all_ref[pl.ds(COEF_AT + at, HALO), :], zero], axis=0)


def strip_kernel(x_hbm, coef_hbm, spacing_hbm, all_ref, cross_ref, twin_ref, x_ref, sems):
    some = PLANES // PARTS
    copies = [
        pltpu.make_async_copy(coef_hbm, all_ref.at[pl.ds(COEF_AT, ROWS)], sems.at[PARTS]),
        pltpu.make_async_copy(spacing_hbm, all_ref.at[pl.ds(SPACING_AT, ROWS)], sems.at[PARTS + 1]),
    ]
    for k in range(PARTS):
        piece = pl.ds(k * some, some)
        copies.append(pltpu.make_async_copy(x_hbm.at[piece], x_ref.at[piece], sems.at[k]))
    for copy in copies[2:] + copies[:2]:
        copy.start()
    for k in range(PARTS):
        copies[k + 2].wait()
        piece = x_ref[pl.ds(k * some, some)].astype(F32)
        all_ref[pl.ds(k * some * ROWS, some * ROWS), :] = piece.reshape(some * ROWS, COLS)
    copies[0].wait()
    copies[1].wait()
    row, col = iota((2 * HALO, COLS), 0), iota((2 * HALO, COLS), 1)
    pick = (col == jnp.where(row < HALO, row, COLS - 2 * HALO + row)).astype(BF16)
    even = lax.axis_index("normal") % 2 == 0
    coef = all_ref[pl.ds(COEF_AT, ROWS), :]
    coef_t = jnp.transpose(jnp.concatenate([coef, jnp.zeros((COLS - ROWS, COLS), F32)], axis=0))
    ends = jnp.concatenate([coef_t[:HALO], coef_t[COLS - HALO :]], axis=0)
    pad = jnp.zeros((COLS - PLANES, COLS), BF16)
    for i in range(ROWS):
        planes = all_ref[pl.ds(i, PLANES, stride=ROWS), :]
        strip = nt(pick, jnp.concatenate([planes.astype(BF16), pad], axis=0))
        strip = jnp.where(col < PLANES, strip, jnp.broadcast_to(ends[:, i : i + 1], (2 * HALO, COLS)))
        cross_ref[i] = jnp.where(even, strip[:HALO], strip[HALO:])
        twin_ref[i] = jnp.where(even, strip[HALO:], strip[:HALO])


def pass_kernel(ref, out_ref):
    out_ref[...] = ref[...]


def corner_kernel(cross, twin, top, bottom, strips_ref, top_ref, bottom_ref):
    even = lax.axis_index("normal") % 2 == 0
    right = jnp.where(even, twin[...], cross[...])
    left = jnp.where(even, cross[...], twin[...])
    strips = jnp.concatenate([right, left], axis=1)
    strips_ref[...] = strips
    top_ref[pl.ds(0, MAIN), :] = top[...]
    bottom_ref[pl.ds(0, MAIN), :] = bottom[...]
    for r in range(HALO - 1):
        top_ref[pl.ds(MAIN + 8 * r, 8), :] = strips[r]
        bottom_ref[pl.ds(MAIN + 8 * r, 8), :] = strips[ROWS - HALO + 1 + r]


def setup_kernel(all_ref, after_corner, v, f, weights, sums, ct):
    select = selector()
    ring_coef = masked_ring(all_ref[pl.ds(COEF_AT, ROWS), :], ct)
    for r in range(ROWS):
        v[pl.ds(r * WIDE, WIDE), :] = to_lanes(select, all_ref[pl.ds(r, PLANES, stride=ROWS), :])
        f[pl.ds(r * WIDE, WIDE), :] = jnp.broadcast_to(ring_coef[:, r : r + 1], (WIDE, COLS))
    spacing = all_ref[pl.ds(SPACING_AT, ROWS), :]
    earlier = (iota((COLS, COLS), 0) < iota((COLS, COLS), 1)).astype(F32)
    before = lax.dot_general(
        spacing, earlier, (((1,), (0,)), ((), ())), preferred_element_type=F32, precision=lax.Precision.HIGHEST
    )
    s_high, s_low = split(spacing)
    q_high, q_low = split(before * spacing)
    weights[...] = jnp.concatenate([s_high, q_high, s_low, q_low], axis=0)
    total = jnp.broadcast_to(jnp.sum(spacing, axis=1, keepdims=True), (ROWS, COLS))
    empty = jnp.zeros((ROWS, COLS), F32)
    sums[...] = jnp.concatenate([empty, empty, total, empty], axis=0)


def inner_kernel(v_in, f_in, strips, weights, sums_in, v, f, kept, part, sums):
    for r in range(ROWS):
        put_strip(v, r, strips[r])
        put_strip(f, r, coef_strip(strips[r]))

    for sweep in range(SWEEPS):
        put = put_line if sweep < SWEEPS - 1 else put_plain
        low, high = sweep + 1, ROWS - 2 - sweep

        def step(r, held):
            sofar, here = held
            value = line_of(v, r + 1)
            after = line_of(f, r + 1) * value
            put(v, r, sofar + after)
            return opened(value, after, here), after

        value = line_of(v, low)
        here = line_of(f, low) * value
        put_line(kept, sweep, here)
        held = (opened(value, here, line_of(f, low - 1) * line_of(v, low - 1)), here)
        held = lax.fori_loop(low, high, step, held, unroll=8)
        put_line(kept, HALO + sweep, held[1])
        put(v, high, held[0] + line_of(f, high + 1) * line_of(v, high + 1))

    sums[...] = sums_in[...]
    eye = (iota((PLANES, COLS), 0) == iota((PLANES, COLS), 1)).astype(BF16)
    for i in range(HALO, ROWS - HALO):
        high, p, q = line_sums(v[pl.ds(i * WIDE, COLS), :], weight_of(weights[...], i))
        sums[pl.ds(i, 1), :] = p
        sums[pl.ds(ROWS + i, 1), :] = q
        part[pl.ds(i, PLANES, stride=ROWS), :] = nt(eye, high)


def outer_kernel(above, below, v, f, kept, sums_in, weights, xe, send_ref, hv, hf, ct, plain, sums):
    select = selector()
    ring_coef = masked_ring(jnp.concatenate([above[pl.ds(COEFS, HALO), :], below[pl.ds(COEFS, HALO), :]], axis=0), ct)
    for k in range(HALO):
        for message, at, c, sent in ((above, k, k, k - 1), (below, 3 * HALO + k, HALO + k, k)):
            hv[pl.ds(at * WIDE, WIDE), :] = to_lanes(select, message[pl.ds(k * PLANES, PLANES), :])
            hf[pl.ds(at * WIDE, WIDE), :] = jnp.broadcast_to(ring_coef[:, c : c + 1], (WIDE, COLS))
            strip = message[pl.ds(MAIN + 8 * sent, 8), :] if 0 <= sent < HALO - 1 else jnp.zeros((8, COLS), F32)
            put_strip(hv, at, strip)
            put_strip(hf, at, coef_strip(strip))
    own = {HALO + k: k for k in range(HALO)} | {2 * HALO + k: ROWS - HALO + k for k in range(HALO)}
    moved = set()

    def value_of(e):
        return line_of(v, own[e]) if e in own and e not in moved else line_of(hv, e)

    def coef_of(e):
        return line_of(f, own[e]) if e in own else line_of(hf, e)

    def chain(first, before, last_after):
        value = value_of(first)
        here = coef_of(first) * value
        sofar = opened(value, here, before)
        for e in range(first, first + HALO):
            if e == first + HALO - 1 and last_after is not None:
                put_line(hv, e, sofar + last_after)
            else:
                value = value_of(e + 1)
                after = coef_of(e + 1) * value
                put_line(hv, e, sofar + after)
                if e < first + HALO - 1:
                    sofar = opened(value, after, here)
                here = after
            moved.add(e)

    for sweep in range(SWEEPS):
        chain(sweep + 1, coef_of(sweep) * value_of(sweep), line_of(kept, sweep))
        chain(3 * HALO - 1 - sweep, line_of(kept, HALO + sweep), None)
    sums[...] = sums_in[...]
    eye = (iota((PLANES, COLS), 0) == iota((PLANES, COLS), 1)).astype(BF16)
    for k in range(2 * HALO):
        i = k if k < HALO else ROWS - 2 * HALO + k
        put_plain(plain, k, line_of(hv, HALO + k))
        high, p, q = line_sums(plain[pl.ds(k * WIDE, COLS), :], weight_of(weights[...], i))
        sums[pl.ds(i, 1), :] = p
        sums[pl.ds(ROWS + i, 1), :] = q
        xe[pl.ds(k, PLANES, stride=2 * HALO), :] = nt(eye, high)
    sums[...] = jnp.transpose(sums[...])
    owners = send_ref.shape[0]
    each = LAYER // owners
    for c in range(3):
        for e in range(each):
            send_ref[:, c * each + e, :] = sums[pl.ds(c * LAYER + e, owners, stride=each), :]
    send_ref[:, 3 * each :, :] = jnp.zeros((owners, 8 - 3 * each, COLS), F32)


def final_kernel(got_ref, part, xe, out_ref, wall_ref):
    tiles = part[pl.ds(0, PLANES * ROWS), :].reshape(PLANES, ROWS // 8, 8, COLS)
    ends = xe[pl.ds(0, PLANES * 8), :].reshape(PLANES, 8, COLS)
    near = iota((PLANES, 8, COLS), 1) < HALO
    head = jnp.where(near, ends, tiles[:, 0])
    tail = jnp.where(near, tiles[:, 3], ends)
    out_ref[...] = jnp.concatenate([head, tiles[:, 1], tiles[:, 2], tail], axis=1).astype(BF16)
    owners = got_ref.shape[0]
    each = LAYER // owners
    own = [pltpu.roll(got_ref[d], COLS - 2 * ROWS, 1) for d in range(owners)]
    total = own[0]
    for d in range(1, owners):
        total = total + own[d]
    rest = total
    acc = jnp.zeros_like(total)
    moment = jnp.zeros_like(total)
    for d in range(owners):
        acc = acc + got_ref[d] * rest
        moment = moment + got_ref[d]
        rest = rest - own[d]
    acc = acc - pltpu.roll(moment, COLS - ROWS, 1)
    value = (acc / total) / total * math.sqrt(COLS * owners)
    for c in range(3):
        wall_ref[c] = value[c * each : (c + 1) * each, :ROWS]


def shaped(*shape):
    return jax.ShapeDtypeStruct(shape, F32)


def lines(count):
    return pltpu.VMEM((count * WIDE + SPARE, COLS), F32)


def body(adjoint_in, coef, spacing):
    wraps, owners = lax.axis_size("wrap"), lax.axis_size("normal")
    strip, square = shaped(ROWS, HALO, COLS), shaped(COLS, COLS)
    own_rows = shaped(ROWS * WIDE + SPARE, COLS)
    x = adjoint_in.reshape(PLANES, ROWS, COLS)
    everything, to_cross, to_twin = call(
        strip_kernel,
        [HBM] * 3,
        [shaped(ALL, COLS), strip, strip],
        [pltpu.VMEM((PLANES, ROWS, COLS), BF16), pltpu.SemaphoreType.DMA((PARTS + 2,))],
        1_000,
    )(*[pltpu.with_memory_space_constraint(a, pltpu.HBM) for a in (x, coef, spacing)])
    to_twin = call(pass_kernel, 1, strip, [], 1_000)(to_twin)
    cross = lax.ppermute(to_cross, "normal", [(k, k + 1 if k % 2 else k - 1) for k in range(1, owners - 1)])
    cross = call(pass_kernel, 1, strip, [], 1_000)(cross)
    twin = lax.ppermute(to_twin, "normal", [(k, k ^ 1) for k in range(owners)])
    top, bottom = call(rows_kernel, 2, [shaped(MAIN, COLS)] * 2, [], 1_000)(everything, to_twin)
    strips, top, bottom = call(corner_kernel, 4, [shaped(ROWS, 8, COLS), shaped(MSG, COLS), shaped(MSG, COLS)], [], 1_000)(
        cross, twin, top, bottom
    )
    v, f, weights, sums = call(
        setup_kernel, 2, [own_rows, own_rows, square, square], [pltpu.VMEM((WIDE + SPARE, COLS), F32)], 1_000
    )(everything, strips)
    above = lax.ppermute(bottom, "wrap", [(k, (k + 1) % wraps) for k in range(wraps)])
    below = lax.ppermute(top, "wrap", [((k + 1) % wraps, k) for k in range(wraps)])
    v, f, kept, part, sums = call(
        inner_kernel,
        5,
        [own_rows, own_rows, shaped(2 * HALO * WIDE, COLS), shaped(PLANES * ROWS + ROWS, COLS), square],
        [],
        20_000_000_000,
        {0: 0, 1: 1},
    )(v, f, strips, weights, sums)
    ends, sums = call(
        outer_kernel,
        7,
        [shaped(PLANES * 2 * HALO + 2 * HALO, COLS), shaped(owners, 8, COLS)],
        [lines(4 * HALO), lines(4 * HALO), pltpu.VMEM((WIDE + SPARE, COLS), F32), lines(2 * HALO), pltpu.VMEM((COLS, COLS), F32)],
        1_000,
    )(above, below, v, f, kept, sums, weights)
    got = lax.all_to_all(sums, "normal", 0, 0, tiled=True)
    adjoint_out, wall_sens = call(
        final_kernel,
        3,
        [jax.ShapeDtypeStruct((PLANES, ROWS, COLS), BF16), shaped(3, LAYER // owners, ROWS)],
        [],
        1_000,
    )(got, part, ends)
    return adjoint_out.reshape(3, LAYER, ROWS, COLS), wall_sens


def solution(mesh):
    placed = (P(None, None, "wrap", "normal"), P("wrap", "normal"), P("wrap", "normal"))
    return jax.shard_map(
        body,
        mesh=mesh,
        in_specs=placed,
        out_specs=(P(None, None, "wrap", "normal"), P(None, "normal", "wrap")),
        check_vma=False,
    )
```

```python
import math

import jax
import jax.numpy as jnp
from jax import lax
from jax.experimental import pallas as pl
from jax.experimental.pallas import tpu as pltpu
from jax.sharding import PartitionSpec as P

SWEEPS = 4
HALO = 4
PLANES = 96
LAYER = 32
ROWS = 32
COLS = 128
WIDE = COLS + 2 * HALO
STEPS = WIDE // 8
STRIP_AT = WIDE - 7 * 8 - 1
COEFS = HALO * PLANES
MAIN = COEFS + 8
MSG = MAIN + 8 * (HALO - 1)
SPARE = 3 * 8
F32 = jnp.float32
BF16 = jnp.bfloat16
COEF_AT = PLANES * ROWS
SPACING_AT = COEF_AT + ROWS
ALL = SPACING_AT + ROWS
PARTS = 2
VMEM = pl.BlockSpec(memory_space=pltpu.VMEM)
HBM = pl.BlockSpec(memory_space=pltpu.HBM)


def nt(a, b):
    return lax.dot_general(a, b, (((1,), (1,)), ((), ())), preferred_element_type=F32)


def iota(shape, dim):
    return lax.broadcasted_iota(jnp.int32, shape, dim)


def call(kernel, ins, outs, scratch, cost, aliases=None):
    single = not isinstance(outs, (list, tuple))
    return pl.pallas_call(
        kernel,
        in_specs=ins if isinstance(ins, list) else [VMEM] * ins,
        out_shape=outs,
        out_specs=VMEM if single else [VMEM] * len(outs),
        scratch_shapes=scratch,
        input_output_aliases=aliases or {},
        compiler_params=pltpu.CompilerParams(vmem_limit_bytes=24 * 1024 * 1024),
        cost_estimate=pl.CostEstimate(flops=cost, bytes_accessed=1_000, transcendentals=0),
    )


def ring(line):
    return 17 * (line & 7) + (line >> 3)


def line_of(ref, r):
    return ref[pl.ds(pl.multiple_of(r * WIDE, 8), WIDE), :].reshape(STEPS, 8, COLS)


def put_line(ref, r, value):
    ref[pl.ds(pl.multiple_of(r * WIDE, 8), WIDE), :] = value.reshape(WIDE, COLS)


def put_plain(ref, r, value):
    for q in range(STEPS):
        ref[pl.ds(r * WIDE + q, 8, stride=STEPS), :] = value[q]


def put_strip(ref, r, strip):
    ref[pl.ds(r * WIDE + STRIP_AT, 8, stride=8), :] = strip


def opened(value, here, before):
    first = pltpu.roll(here[STEPS - 1], 1, 0)[None]
    last = pltpu.roll(here[0], 7, 0)[None]
    beside = jnp.concatenate([first, here[:-1]], axis=0) + jnp.concatenate([here[1:], last], axis=0)
    return (value - 4.0 * here) + (beside + before)


def selector():
    shape = (WIDE, COLS)
    return (ring(iota(shape, 0)) == iota(shape, 1)).astype(BF16)


def to_lanes(select, planes):
    pad = jnp.zeros((COLS - PLANES, COLS), BF16)
    return nt(select, jnp.concatenate([planes.astype(BF16), pad], axis=0))


def coef_strip(strip):
    return jnp.broadcast_to(strip[:, PLANES : PLANES + 1], (8, COLS))


def masked_ring(coef, scratch):
    rows = coef.shape[0]
    coef_t = jnp.transpose(jnp.concatenate([coef, jnp.zeros((COLS - rows, COLS), F32)], axis=0))
    place, last = lax.axis_index("normal"), lax.axis_size("normal") - 1
    col = iota((COLS, COLS), 0)
    outer = ((col == 0) & (place == 0)) | ((col == COLS - 1) & (place == last))
    scratch[pl.ds(0, COLS), :] = jnp.where(outer, 0.0, coef_t)
    scratch[pl.ds(COLS, 8), :] = jnp.zeros((8, COLS), F32)
    return jnp.concatenate([scratch[pl.ds(q, 8, stride=STEPS), :] for q in range(STEPS)], axis=0)


def line_sums(value, weight):
    high = value.astype(BF16)
    low = (value - high.astype(F32)).astype(BF16)
    both = lax.dot_general(
        jnp.concatenate([weight, weight], axis=1),
        jnp.concatenate([high, low], axis=0),
        (((1,), (0,)), ((), ())),
        preferred_element_type=F32,
    )
    return high, both[0:1] + both[2:3], both[1:2] + both[3:4]


def weight_of(weights, i):
    place = iota((16, COLS), 0)
    rows = [jnp.broadcast_to(weights[k * ROWS + i : k * ROWS + i + 1], (16, COLS)) for k in range(4)]
    rest = jnp.where(place == 2, rows[2], jnp.where(place == 3, rows[3], 0.0))
    return jnp.where(place == 0, rows[0], jnp.where(place == 1, rows[1], rest)).astype(BF16)


def split(value):
    high = value.astype(BF16).astype(F32)
    return high, value - high


def rows_kernel(all_ref, after_twin, top_ref, bottom_ref):
    zero = jnp.zeros((HALO, COLS), F32)
    for ref, at in ((top_ref, 0), (bottom_ref, ROWS - HALO)):
        for k in range(HALO):
            ref[pl.ds(k * PLANES, PLANES), :] = all_ref[pl.ds(at + k, PLANES, stride=ROWS), :]
        ref[pl.ds(COEFS, 8), :] = jnp.concatenate([all_ref[pl.ds(COEF_AT + at, HALO), :], zero], axis=0)


def strip_kernel(x_hbm, coef_hbm, spacing_hbm, all_ref, cross_ref, twin_ref, x_ref, sems):
    some = PLANES // PARTS
    copies = [
        pltpu.make_async_copy(coef_hbm, all_ref.at[pl.ds(COEF_AT, ROWS)], sems.at[PARTS]),
        pltpu.make_async_copy(spacing_hbm, all_ref.at[pl.ds(SPACING_AT, ROWS)], sems.at[PARTS + 1]),
    ]
    for k in range(PARTS):
        piece = pl.ds(k * some, some)
        copies.append(pltpu.make_async_copy(x_hbm.at[piece], x_ref.at[piece], sems.at[k]))
    for copy in copies[2:] + copies[:2]:
        copy.start()
    for k in range(PARTS):
        copies[k + 2].wait()
        piece = x_ref[pl.ds(k * some, some)].astype(F32)
        all_ref[pl.ds(k * some * ROWS, some * ROWS), :] = piece.reshape(some * ROWS, COLS)
    copies[0].wait()
    copies[1].wait()
    row, col = iota((2 * HALO, COLS), 0), iota((2 * HALO, COLS), 1)
    pick = (col == jnp.where(row < HALO, row, COLS - 2 * HALO + row)).astype(BF16)
    even = lax.axis_index("normal") % 2 == 0
    coef = all_ref[pl.ds(COEF_AT, ROWS), :]
    coef_t = jnp.transpose(jnp.concatenate([coef, jnp.zeros((COLS - ROWS, COLS), F32)], axis=0))
    ends = jnp.concatenate([coef_t[:HALO], coef_t[COLS - HALO :]], axis=0)
    pad = jnp.zeros((COLS - PLANES, COLS), BF16)
    for i in range(ROWS):
        planes = all_ref[pl.ds(i, PLANES, stride=ROWS), :]
        strip = nt(pick, jnp.concatenate([planes.astype(BF16), pad], axis=0))
        strip = jnp.where(col < PLANES, strip, jnp.broadcast_to(ends[:, i : i + 1], (2 * HALO, COLS)))
        cross_ref[i] = jnp.where(even, strip[:HALO], strip[HALO:])
        twin_ref[i] = jnp.where(even, strip[HALO:], strip[:HALO])


def pass_kernel(ref, out_ref):
    out_ref[...] = ref[...]


def corner_kernel(cross, twin, top, bottom, strips_ref, top_ref, bottom_ref):
    even = lax.axis_index("normal") % 2 == 0
    right = jnp.where(even, twin[...], cross[...])
    left = jnp.where(even, cross[...], twin[...])
    strips = jnp.concatenate([right, left], axis=1)
    strips_ref[...] = strips
    top_ref[pl.ds(0, MAIN), :] = top[...]
    bottom_ref[pl.ds(0, MAIN), :] = bottom[...]
    for r in range(HALO - 1):
        top_ref[pl.ds(MAIN + 8 * r, 8), :] = strips[r]
        bottom_ref[pl.ds(MAIN + 8 * r, 8), :] = strips[ROWS - HALO + 1 + r]


def setup_kernel(all_ref, after_corner, v, f, weights, sums, ct):
    select = selector()
    ring_coef = masked_ring(all_ref[pl.ds(COEF_AT, ROWS), :], ct)
    for r in range(ROWS):
        v[pl.ds(r * WIDE, WIDE), :] = to_lanes(select, all_ref[pl.ds(r, PLANES, stride=ROWS), :])
        f[pl.ds(r * WIDE, WIDE), :] = jnp.broadcast_to(ring_coef[:, r : r + 1], (WIDE, COLS))
    spacing = all_ref[pl.ds(SPACING_AT, ROWS), :]
    earlier = (iota((COLS, COLS), 0) < iota((COLS, COLS), 1)).astype(F32)
    before = lax.dot_general(
        spacing, earlier, (((1,), (0,)), ((), ())), preferred_element_type=F32, precision=lax.Precision.HIGHEST
    )
    s_high, s_low = split(spacing)
    q_high, q_low = split(before * spacing)
    weights[...] = jnp.concatenate([s_high, q_high, s_low, q_low], axis=0)
    total = jnp.broadcast_to(jnp.sum(spacing, axis=1, keepdims=True), (ROWS, COLS))
    empty = jnp.zeros((ROWS, COLS), F32)
    sums[...] = jnp.concatenate([empty, empty, total, empty], axis=0)


def inner_kernel(v_in, f_in, strips, weights, sums_in, v, f, kept, part, sums):
    for r in range(ROWS):
        put_strip(v, r, strips[r])
        put_strip(f, r, coef_strip(strips[r]))

    for sweep in range(SWEEPS):
        put = put_line if sweep < SWEEPS - 1 else put_plain
        low, high = sweep + 1, ROWS - 2 - sweep

        def step(r, held):
            sofar, here = held
            value = line_of(v, r + 1)
            after = line_of(f, r + 1) * value
            put(v, r, sofar + after)
            return opened(value, after, here), after

        value = line_of(v, low)
        here = line_of(f, low) * value
        put_line(kept, sweep, here)
        held = (opened(value, here, line_of(f, low - 1) * line_of(v, low - 1)), here)
        held = lax.fori_loop(low, high, step, held, unroll=8)
        put_line(kept, HALO + sweep, held[1])
        put(v, high, held[0] + line_of(f, high + 1) * line_of(v, high + 1))

    sums[...] = sums_in[...]
    eye = (iota((PLANES, COLS), 0) == iota((PLANES, COLS), 1)).astype(BF16)
    for i in range(HALO, ROWS - HALO):
        high, p, q = line_sums(v[pl.ds(i * WIDE, COLS), :], weight_of(weights[...], i))
        sums[pl.ds(i, 1), :] = p
        sums[pl.ds(ROWS + i, 1), :] = q
        part[pl.ds(i, PLANES, stride=ROWS), :] = nt(eye, high)


def outer_kernel(above, below, v, f, kept, sums_in, weights, xe, send_ref, hv, hf, ct, plain, sums):
    select = selector()
    ring_coef = masked_ring(jnp.concatenate([above[pl.ds(COEFS, HALO), :], below[pl.ds(COEFS, HALO), :]], axis=0), ct)
    for k in range(HALO):
        for message, at, c, sent in ((above, k, k, k - 1), (below, 3 * HALO + k, HALO + k, k)):
            hv[pl.ds(at * WIDE, WIDE), :] = to_lanes(select, message[pl.ds(k * PLANES, PLANES), :])
            hf[pl.ds(at * WIDE, WIDE), :] = jnp.broadcast_to(ring_coef[:, c : c + 1], (WIDE, COLS))
            strip = message[pl.ds(MAIN + 8 * sent, 8), :] if 0 <= sent < HALO - 1 else jnp.zeros((8, COLS), F32)
            put_strip(hv, at, strip)
            put_strip(hf, at, coef_strip(strip))
    own = {HALO + k: k for k in range(HALO)} | {2 * HALO + k: ROWS - HALO + k for k in range(HALO)}
    moved = set()

    def value_of(e):
        return line_of(v, own[e]) if e in own and e not in moved else line_of(hv, e)

    def coef_of(e):
        return line_of(f, own[e]) if e in own else line_of(hf, e)

    def chain(first, before, last_after):
        value = value_of(first)
        here = coef_of(first) * value
        sofar = opened(value, here, before)
        for e in range(first, first + HALO):
            if e == first + HALO - 1 and last_after is not None:
                put_line(hv, e, sofar + last_after)
            else:
                value = value_of(e + 1)
                after = coef_of(e + 1) * value
                put_line(hv, e, sofar + after)
                if e < first + HALO - 1:
                    sofar = opened(value, after, here)
                here = after
            moved.add(e)

    for sweep in range(SWEEPS):
        chain(sweep + 1, coef_of(sweep) * value_of(sweep), line_of(kept, sweep))
        chain(3 * HALO - 1 - sweep, line_of(kept, HALO + sweep), None)
    sums[...] = sums_in[...]
    for k in range(2 * HALO):
        i = k if k < HALO else ROWS - 2 * HALO + k
        put_plain(plain, k, line_of(hv, HALO + k))
        high, p, q = line_sums(plain[pl.ds(k * WIDE, COLS), :], weight_of(weights[...], i))
        sums[pl.ds(i, 1), :] = p
        sums[pl.ds(ROWS + i, 1), :] = q
        turned = jnp.transpose(high.astype(F32))[:PLANES]
        xe[pl.ds(k, PLANES, stride=2 * HALO), :] = turned
    sums[...] = jnp.transpose(sums[...])
    owners = send_ref.shape[0]
    each = LAYER // owners
    for c in range(3):
        for e in range(each):
            send_ref[:, c * each + e, :] = sums[pl.ds(c * LAYER + e, owners, stride=each), :]
    send_ref[:, 3 * each :, :] = jnp.zeros((owners, 8 - 3 * each, COLS), F32)


def final_kernel(got_ref, part, xe, out_ref, wall_ref):
    tiles = part[pl.ds(0, PLANES * ROWS), :].reshape(PLANES, ROWS // 8, 8, COLS)
    ends = xe[pl.ds(0, PLANES * 8), :].reshape(PLANES, 8, COLS)
    near = iota((PLANES, 8, COLS), 1) < HALO
    head = jnp.where(near, ends, tiles[:, 0])
    tail = jnp.where(near, tiles[:, 3], ends)
    out_ref[...] = jnp.concatenate([head, tiles[:, 1], tiles[:, 2], tail], axis=1).astype(BF16)
    owners = got_ref.shape[0]
    each = LAYER // owners
    own = [pltpu.roll(got_ref[d], COLS - 2 * ROWS, 1) for d in range(owners)]
    total = own[0]
    for d in range(1, owners):
        total = total + own[d]
    rest = total
    acc = jnp.zeros_like(total)
    moment = jnp.zeros_like(total)
    for d in range(owners):
        acc = acc + got_ref[d] * rest
        moment = moment + got_ref[d]
        rest = rest - own[d]
    acc = acc - pltpu.roll(moment, COLS - ROWS, 1)
    value = (acc / total) / total * math.sqrt(COLS * owners)
    for c in range(3):
        wall_ref[c] = value[c * each : (c + 1) * each, :ROWS]


def shaped(*shape):
    return jax.ShapeDtypeStruct(shape, F32)


def lines(count):
    return pltpu.VMEM((count * WIDE + SPARE, COLS), F32)


def body(adjoint_in, coef, spacing):
    wraps, owners = lax.axis_size("wrap"), lax.axis_size("normal")
    strip, square = shaped(ROWS, HALO, COLS), shaped(COLS, COLS)
    own_rows = shaped(ROWS * WIDE + SPARE, COLS)
    x = adjoint_in.reshape(PLANES, ROWS, COLS)
    everything, to_cross, to_twin = call(
        strip_kernel,
        [HBM] * 3,
        [shaped(ALL, COLS), strip, strip],
        [pltpu.VMEM((PLANES, ROWS, COLS), BF16), pltpu.SemaphoreType.DMA((PARTS + 2,))],
        1_000,
    )(*[pltpu.with_memory_space_constraint(a, pltpu.HBM) for a in (x, coef, spacing)])
    to_twin = call(pass_kernel, 1, strip, [], 1_000)(to_twin)
    cross = lax.ppermute(to_cross, "normal", [(k, k + 1 if k % 2 else k - 1) for k in range(1, owners - 1)])
    cross = call(pass_kernel, 1, strip, [], 1_000)(cross)
    twin = lax.ppermute(to_twin, "normal", [(k, k ^ 1) for k in range(owners)])
    top, bottom = call(rows_kernel, 2, [shaped(MAIN, COLS)] * 2, [], 1_000)(everything, to_twin)
    strips, top, bottom = call(corner_kernel, 4, [shaped(ROWS, 8, COLS), shaped(MSG, COLS), shaped(MSG, COLS)], [], 1_000)(
        cross, twin, top, bottom
    )
    v, f, weights, sums = call(
        setup_kernel, 2, [own_rows, own_rows, square, square], [pltpu.VMEM((WIDE + SPARE, COLS), F32)], 1_000
    )(everything, strips)
    above = lax.ppermute(bottom, "wrap", [(k, (k + 1) % wraps) for k in range(wraps)])
    below = lax.ppermute(top, "wrap", [((k + 1) % wraps, k) for k in range(wraps)])
    v, f, kept, part, sums = call(
        inner_kernel,
        5,
        [own_rows, own_rows, shaped(2 * HALO * WIDE, COLS), shaped(PLANES * ROWS + ROWS, COLS), square],
        [],
        20_000_000_000,
        {0: 0, 1: 1},
    )(v, f, strips, weights, sums)
    ends, sums = call(
        outer_kernel,
        7,
        [shaped(PLANES * 2 * HALO + 2 * HALO, COLS), shaped(owners, 8, COLS)],
        [lines(4 * HALO), lines(4 * HALO), pltpu.VMEM((WIDE + SPARE, COLS), F32), lines(2 * HALO), pltpu.VMEM((COLS, COLS), F32)],
        1_000,
    )(above, below, v, f, kept, sums, weights)
    got = lax.all_to_all(sums, "normal", 0, 0, tiled=True)
    adjoint_out, wall_sens = call(
        final_kernel,
        3,
        [jax.ShapeDtypeStruct((PLANES, ROWS, COLS), BF16), shaped(3, LAYER // owners, ROWS)],
        [],
        1_000,
    )(got, part, ends)
    return adjoint_out.reshape(3, LAYER, ROWS, COLS), wall_sens


def solution(mesh):
    placed = (P(None, None, "wrap", "normal"), P("wrap", "normal"), P("wrap", "normal"))
    return jax.shard_map(
        body,
        mesh=mesh,
        in_specs=placed,
        out_specs=(P(None, None, "wrap", "normal"), P(None, "normal", "wrap")),
        check_vma=False,
    )
```

```python
import math

import jax
import jax.numpy as jnp
from jax import lax
from jax.experimental import pallas as pl
from jax.experimental.pallas import tpu as pltpu
from jax.sharding import PartitionSpec as P

SWEEPS = 4
HALO = 4
PLANES = 96
LAYER = 32
ROWS = 32
COLS = 128
WIDE = COLS + 2 * HALO
STEPS = WIDE // 8
STRIP_AT = WIDE - 7 * 8 - 1
COEFS = HALO * PLANES
MAIN = COEFS + 8
MSG = MAIN + 8 * (HALO - 1)
SPARE = 3 * 8
F32 = jnp.float32
BF16 = jnp.bfloat16
COEF_AT = PLANES * ROWS
SPACING_AT = COEF_AT + ROWS
ALL = SPACING_AT + ROWS
PARTS = 2
VMEM = pl.BlockSpec(memory_space=pltpu.VMEM)
HBM = pl.BlockSpec(memory_space=pltpu.HBM)


def nt(a, b):
    return lax.dot_general(a, b, (((1,), (1,)), ((), ())), preferred_element_type=F32)


def iota(shape, dim):
    return lax.broadcasted_iota(jnp.int32, shape, dim)


def call(kernel, ins, outs, scratch, cost, aliases=None):
    single = not isinstance(outs, (list, tuple))
    return pl.pallas_call(
        kernel,
        in_specs=ins if isinstance(ins, list) else [VMEM] * ins,
        out_shape=outs,
        out_specs=VMEM if single else [VMEM] * len(outs),
        scratch_shapes=scratch,
        input_output_aliases=aliases or {},
        compiler_params=pltpu.CompilerParams(vmem_limit_bytes=24 * 1024 * 1024),
        cost_estimate=pl.CostEstimate(flops=cost, bytes_accessed=1_000, transcendentals=0),
    )


def ring(line):
    return 17 * (line & 7) + (line >> 3)


def line_of(ref, r):
    return ref[pl.ds(pl.multiple_of(r * WIDE, 8), WIDE), :].reshape(STEPS, 8, COLS)


def put_line(ref, r, value):
    ref[pl.ds(pl.multiple_of(r * WIDE, 8), WIDE), :] = value.reshape(WIDE, COLS)


def put_plain(ref, r, value):
    for q in range(STEPS):
        ref[pl.ds(r * WIDE + q, 8, stride=STEPS), :] = value[q]


def put_strip(ref, r, strip):
    ref[pl.ds(r * WIDE + STRIP_AT, 8, stride=8), :] = strip


def opened(value, here, before):
    first = pltpu.roll(here[STEPS - 1], 1, 0)[None]
    last = pltpu.roll(here[0], 7, 0)[None]
    beside = jnp.concatenate([first, here[:-1]], axis=0) + jnp.concatenate([here[1:], last], axis=0)
    return (value - 4.0 * here) + (beside + before)


def selector():
    shape = (WIDE, COLS)
    return (ring(iota(shape, 0)) == iota(shape, 1)).astype(BF16)


def to_lanes(select, planes):
    pad = jnp.zeros((COLS - PLANES, COLS), BF16)
    return nt(select, jnp.concatenate([planes.astype(BF16), pad], axis=0))


def coef_strip(strip):
    return jnp.broadcast_to(strip[:, PLANES : PLANES + 1], (8, COLS))


def masked_ring(coef, scratch):
    rows = coef.shape[0]
    coef_t = jnp.transpose(jnp.concatenate([coef, jnp.zeros((COLS - rows, COLS), F32)], axis=0))
    place, last = lax.axis_index("normal"), lax.axis_size("normal") - 1
    col = iota((COLS, COLS), 0)
    outer = ((col == 0) & (place == 0)) | ((col == COLS - 1) & (place == last))
    scratch[pl.ds(0, COLS), :] = jnp.where(outer, 0.0, coef_t)
    scratch[pl.ds(COLS, 8), :] = jnp.zeros((8, COLS), F32)
    return jnp.concatenate([scratch[pl.ds(q, 8, stride=STEPS), :] for q in range(STEPS)], axis=0)


def line_sums(value, weight):
    high = value.astype(BF16)
    low = (value - high.astype(F32)).astype(BF16)
    both = lax.dot_general(
        jnp.concatenate([weight, weight], axis=1),
        jnp.concatenate([high, low], axis=0),
        (((1,), (0,)), ((), ())),
        preferred_element_type=F32,
    )
    return high, both[0:1] + both[2:3], both[1:2] + both[3:4]


def weight_of(weights, i):
    place = iota((16, COLS), 0)
    rows = [jnp.broadcast_to(weights[k * ROWS + i : k * ROWS + i + 1], (16, COLS)) for k in range(4)]
    rest = jnp.where(place == 2, rows[2], jnp.where(place == 3, rows[3], 0.0))
    return jnp.where(place == 0, rows[0], jnp.where(place == 1, rows[1], rest)).astype(BF16)


def split(value):
    high = value.astype(BF16).astype(F32)
    return high, value - high


def rows_kernel(all_ref, after_twin, top_ref, bottom_ref):
    zero = jnp.zeros((HALO, COLS), F32)
    for ref, at in ((top_ref, 0), (bottom_ref, ROWS - HALO)):
        for k in range(HALO):
            ref[pl.ds(k * PLANES, PLANES), :] = all_ref[pl.ds(at + k, PLANES, stride=ROWS), :]
        ref[pl.ds(COEFS, 8), :] = jnp.concatenate([all_ref[pl.ds(COEF_AT + at, HALO), :], zero], axis=0)


def strip_kernel(x_hbm, coef_hbm, spacing_hbm, all_ref, cross_ref, twin_ref, x_ref, sems):
    some = PLANES // PARTS
    copies = [
        pltpu.make_async_copy(coef_hbm, all_ref.at[pl.ds(COEF_AT, ROWS)], sems.at[PARTS]),
        pltpu.make_async_copy(spacing_hbm, all_ref.at[pl.ds(SPACING_AT, ROWS)], sems.at[PARTS + 1]),
    ]
    for k in range(PARTS):
        piece = pl.ds(k * some, some)
        copies.append(pltpu.make_async_copy(x_hbm.at[piece], x_ref.at[piece], sems.at[k]))
    for copy in copies:
        copy.start()
    copies[0].wait()
    coef = all_ref[pl.ds(COEF_AT, ROWS), :]
    coef_t = jnp.transpose(jnp.concatenate([coef, jnp.zeros((COLS - ROWS, COLS), F32)], axis=0))
    ends = jnp.concatenate([coef_t[:HALO], coef_t[COLS - HALO :]], axis=0)
    for k in range(PARTS):
        copies[k + 2].wait()
        piece = x_ref[pl.ds(k * some, some)].astype(F32)
        all_ref[pl.ds(k * some * ROWS, some * ROWS), :] = piece.reshape(some * ROWS, COLS)
    copies[1].wait()
    row, col = iota((2 * HALO, COLS), 0), iota((2 * HALO, COLS), 1)
    pick = (col == jnp.where(row < HALO, row, COLS - 2 * HALO + row)).astype(BF16)
    even = lax.axis_index("normal") % 2 == 0
    pad = jnp.zeros((COLS - PLANES, COLS), BF16)
    for i in range(ROWS):
        planes = all_ref[pl.ds(i, PLANES, stride=ROWS), :]
        strip = nt(pick, jnp.concatenate([planes.astype(BF16), pad], axis=0))
        strip = jnp.where(col < PLANES, strip, jnp.broadcast_to(ends[:, i : i + 1], (2 * HALO, COLS)))
        cross_ref[i] = jnp.where(even, strip[:HALO], strip[HALO:])
        twin_ref[i] = jnp.where(even, strip[HALO:], strip[:HALO])


def pass_kernel(ref, out_ref):
    out_ref[...] = ref[...]


def corner_kernel(cross, twin, top, bottom, strips_ref, top_ref, bottom_ref):
    even = lax.axis_index("normal") % 2 == 0
    right = jnp.where(even, twin[...], cross[...])
    left = jnp.where(even, cross[...], twin[...])
    strips = jnp.concatenate([right, left], axis=1)
    strips_ref[...] = strips
    top_ref[pl.ds(0, MAIN), :] = top[...]
    bottom_ref[pl.ds(0, MAIN), :] = bottom[...]
    for r in range(HALO - 1):
        top_ref[pl.ds(MAIN + 8 * r, 8), :] = strips[r]
        bottom_ref[pl.ds(MAIN + 8 * r, 8), :] = strips[ROWS - HALO + 1 + r]


def setup_kernel(all_ref, after_corner, v, f, weights, sums, ct):
    select = selector()
    ring_coef = masked_ring(all_ref[pl.ds(COEF_AT, ROWS), :], ct)
    for r in range(ROWS):
        v[pl.ds(r * WIDE, WIDE), :] = to_lanes(select, all_ref[pl.ds(r, PLANES, stride=ROWS), :])
        f[pl.ds(r * WIDE, WIDE), :] = jnp.broadcast_to(ring_coef[:, r : r + 1], (WIDE, COLS))
    spacing = all_ref[pl.ds(SPACING_AT, ROWS), :]
    earlier = (iota((COLS, COLS), 0) < iota((COLS, COLS), 1)).astype(F32)
    before = lax.dot_general(
        spacing, earlier, (((1,), (0,)), ((), ())), preferred_element_type=F32, precision=lax.Precision.HIGHEST
    )
    s_high, s_low = split(spacing)
    q_high, q_low = split(before * spacing)
    weights[...] = jnp.concatenate([s_high, q_high, s_low, q_low], axis=0)
    total = jnp.broadcast_to(jnp.sum(spacing, axis=1, keepdims=True), (ROWS, COLS))
    empty = jnp.zeros((ROWS, COLS), F32)
    sums[...] = jnp.concatenate([empty, empty, total, empty], axis=0)


def inner_kernel(v_in, f_in, strips, weights, sums_in, v, f, kept, part, sums):
    for r in range(ROWS):
        put_strip(v, r, strips[r])
        put_strip(f, r, coef_strip(strips[r]))

    for sweep in range(SWEEPS):
        put = put_line if sweep < SWEEPS - 1 else put_plain
        low, high = sweep + 1, ROWS - 2 - sweep

        def step(r, held):
            sofar, here = held
            value = line_of(v, r + 1)
            after = line_of(f, r + 1) * value
            put(v, r, sofar + after)
            return opened(value, after, here), after

        value = line_of(v, low)
        here = line_of(f, low) * value
        put_line(kept, sweep, here)
        held = (opened(value, here, line_of(f, low - 1) * line_of(v, low - 1)), here)
        held = lax.fori_loop(low, high, step, held, unroll=8)
        put_line(kept, HALO + sweep, held[1])
        put(v, high, held[0] + line_of(f, high + 1) * line_of(v, high + 1))

    sums[...] = sums_in[...]
    eye = (iota((PLANES, COLS), 0) == iota((PLANES, COLS), 1)).astype(BF16)
    for i in range(HALO, ROWS - HALO):
        high, p, q = line_sums(v[pl.ds(i * WIDE, COLS), :], weight_of(weights[...], i))
        sums[pl.ds(i, 1), :] = p
        sums[pl.ds(ROWS + i, 1), :] = q
        part[pl.ds(i, PLANES, stride=ROWS), :] = nt(eye, high)


def outer_kernel(above, below, v, f, kept, sums_in, weights, xe, send_ref, hv, hf, ct, plain, sums):
    select = selector()
    ring_coef = masked_ring(jnp.concatenate([above[pl.ds(COEFS, HALO), :], below[pl.ds(COEFS, HALO), :]], axis=0), ct)
    for k in range(HALO):
        for message, at, c, sent in ((above, k, k, k - 1), (below, 3 * HALO + k, HALO + k, k)):
            hv[pl.ds(at * WIDE, WIDE), :] = to_lanes(select, message[pl.ds(k * PLANES, PLANES), :])
            hf[pl.ds(at * WIDE, WIDE), :] = jnp.broadcast_to(ring_coef[:, c : c + 1], (WIDE, COLS))
            strip = message[pl.ds(MAIN + 8 * sent, 8), :] if 0 <= sent < HALO - 1 else jnp.zeros((8, COLS), F32)
            put_strip(hv, at, strip)
            put_strip(hf, at, coef_strip(strip))
    own = {HALO + k: k for k in range(HALO)} | {2 * HALO + k: ROWS - HALO + k for k in range(HALO)}
    moved = set()

    def value_of(e):
        return line_of(v, own[e]) if e in own and e not in moved else line_of(hv, e)

    def coef_of(e):
        return line_of(f, own[e]) if e in own else line_of(hf, e)

    def chain(first, before, last_after):
        value = value_of(first)
        here = coef_of(first) * value
        sofar = opened(value, here, before)
        for e in range(first, first + HALO):
            if e == first + HALO - 1 and last_after is not None:
                put_line(hv, e, sofar + last_after)
            else:
                value = value_of(e + 1)
                after = coef_of(e + 1) * value
                put_line(hv, e, sofar + after)
                if e < first + HALO - 1:
                    sofar = opened(value, after, here)
                here = after
            moved.add(e)

    for sweep in range(SWEEPS):
        chain(sweep + 1, coef_of(sweep) * value_of(sweep), line_of(kept, sweep))
        chain(3 * HALO - 1 - sweep, line_of(kept, HALO + sweep), None)
    sums[...] = sums_in[...]
    eye = (iota((PLANES, COLS), 0) == iota((PLANES, COLS), 1)).astype(BF16)
    for k in range(2 * HALO):
        i = k if k < HALO else ROWS - 2 * HALO + k
        put_plain(plain, k, line_of(hv, HALO + k))
        high, p, q = line_sums(plain[pl.ds(k * WIDE, COLS), :], weight_of(weights[...], i))
        sums[pl.ds(i, 1), :] = p
        sums[pl.ds(ROWS + i, 1), :] = q
        xe[pl.ds(k, PLANES, stride=2 * HALO), :] = nt(eye, high)
    sums[...] = jnp.transpose(sums[...])
    owners = send_ref.shape[0]
    each = LAYER // owners
    for c in range(3):
        for e in range(each):
            send_ref[:, c * each + e, :] = sums[pl.ds(c * LAYER + e, owners, stride=each), :]
    send_ref[:, 3 * each :, :] = jnp.zeros((owners, 8 - 3 * each, COLS), F32)


def final_kernel(got_ref, part, xe, out_ref, wall_ref):
    tiles = part[pl.ds(0, PLANES * ROWS), :].reshape(PLANES, ROWS // 8, 8, COLS)
    ends = xe[pl.ds(0, PLANES * 8), :].reshape(PLANES, 8, COLS)
    near = iota((PLANES, 8, COLS), 1) < HALO
    head = jnp.where(near, ends, tiles[:, 0])
    tail = jnp.where(near, tiles[:, 3], ends)
    out_ref[...] = jnp.concatenate([head, tiles[:, 1], tiles[:, 2], tail], axis=1).astype(BF16)
    owners = got_ref.shape[0]
    each = LAYER // owners
    own = [pltpu.roll(got_ref[d], COLS - 2 * ROWS, 1) for d in range(owners)]
    total = own[0]
    for d in range(1, owners):
        total = total + own[d]
    rest = total
    acc = jnp.zeros_like(total)
    moment = jnp.zeros_like(total)
    for d in range(owners):
        acc = acc + got_ref[d] * rest
        moment = moment + got_ref[d]
        rest = rest - own[d]
    acc = acc - pltpu.roll(moment, COLS - ROWS, 1)
    value = (acc / total) / total * math.sqrt(COLS * owners)
    for c in range(3):
        wall_ref[c] = value[c * each : (c + 1) * each, :ROWS]


def shaped(*shape):
    return jax.ShapeDtypeStruct(shape, F32)


def lines(count):
    return pltpu.VMEM((count * WIDE + SPARE, COLS), F32)


def body(adjoint_in, coef, spacing):
    wraps, owners = lax.axis_size("wrap"), lax.axis_size("normal")
    strip, square = shaped(ROWS, HALO, COLS), shaped(COLS, COLS)
    own_rows = shaped(ROWS * WIDE + SPARE, COLS)
    x = adjoint_in.reshape(PLANES, ROWS, COLS)
    everything, to_cross, to_twin = call(
        strip_kernel,
        [HBM] * 3,
        [shaped(ALL, COLS), strip, strip],
        [pltpu.VMEM((PLANES, ROWS, COLS), BF16), pltpu.SemaphoreType.DMA((PARTS + 2,))],
        1_000,
    )(*[pltpu.with_memory_space_constraint(a, pltpu.HBM) for a in (x, coef, spacing)])
    to_twin = call(pass_kernel, 1, strip, [], 1_000)(to_twin)
    cross = lax.ppermute(to_cross, "normal", [(k, k + 1 if k % 2 else k - 1) for k in range(1, owners - 1)])
    cross = call(pass_kernel, 1, strip, [], 1_000)(cross)
    twin = lax.ppermute(to_twin, "normal", [(k, k ^ 1) for k in range(owners)])
    top, bottom = call(rows_kernel, 2, [shaped(MAIN, COLS)] * 2, [], 1_000)(everything, to_twin)
    strips, top, bottom = call(corner_kernel, 4, [shaped(ROWS, 8, COLS), shaped(MSG, COLS), shaped(MSG, COLS)], [], 1_000)(
        cross, twin, top, bottom
    )
    v, f, weights, sums = call(
        setup_kernel, 2, [own_rows, own_rows, square, square], [pltpu.VMEM((WIDE + SPARE, COLS), F32)], 1_000
    )(everything, strips)
    above = lax.ppermute(bottom, "wrap", [(k, (k + 1) % wraps) for k in range(wraps)])
    below = lax.ppermute(top, "wrap", [((k + 1) % wraps, k) for k in range(wraps)])
    v, f, kept, part, sums = call(
        inner_kernel,
        5,
        [own_rows, own_rows, shaped(2 * HALO * WIDE, COLS), shaped(PLANES * ROWS + ROWS, COLS), square],
        [],
        20_000_000_000,
        {0: 0, 1: 1},
    )(v, f, strips, weights, sums)
    ends, sums = call(
        outer_kernel,
        7,
        [shaped(PLANES * 2 * HALO + 2 * HALO, COLS), shaped(owners, 8, COLS)],
        [lines(4 * HALO), lines(4 * HALO), pltpu.VMEM((WIDE + SPARE, COLS), F32), lines(2 * HALO), pltpu.VMEM((COLS, COLS), F32)],
        1_000,
    )(above, below, v, f, kept, sums, weights)
    got = lax.all_to_all(sums, "normal", 0, 0, tiled=True)
    adjoint_out, wall_sens = call(
        final_kernel,
        3,
        [jax.ShapeDtypeStruct((PLANES, ROWS, COLS), BF16), shaped(3, LAYER // owners, ROWS)],
        [],
        1_000,
    )(got, part, ends)
    return adjoint_out.reshape(3, LAYER, ROWS, COLS), wall_sens


def solution(mesh):
    placed = (P(None, None, "wrap", "normal"), P("wrap", "normal"), P("wrap", "normal"))
    return jax.shard_map(
        body,
        mesh=mesh,
        in_specs=placed,
        out_specs=(P(None, None, "wrap", "normal"), P(None, "normal", "wrap")),
        check_vma=False,
    )
```
